128 devices in a mesh: gx: 16 (over x, z), gy: 8 (over y, core).
Axes of the slice: x: 4, y: 4, z: 4, core: 2. Of those that a mesh axis runs over, the one named last changes fastest.
Arguments:
- state: float32 [144, 128, 1024], P(None, 'gx', 'gy'), may hold values from -6 to 6
- owner: int32 [128, 1024], P('gx', 'gy'), may hold values from 0 to 127, as said below
- counts: int32 [128, 1024], P('gx', 'gy'), may hold values from 1 to 4
- vert: float32 [72, 72], replicated, may hold values from -0.75 to 0.75
- down_map: float32 [50, 72], replicated, may hold values from -0.75 to 0.75
- up_map: float32 [72, 50], replicated, may hold values from -0.875 to 0.875
- courant: float32 [50], replicated, may hold values from 0.05 to 0.9
- crm_field: float32 [3200, 229376], P(None, ('gx', 'gy')), may hold values from -4 to 4
Outputs:
- new_state: float32 [144, 128, 1024], P(None, 'gx', 'gy')
The draws below stay inside these ranges and needn't reach their ends.
Inputs may be any that keep to these rules, and one draw needn't show every extreme that they name: In each device's block of 8 x 128 columns no owner is named more than 14 times; one owner is named exactly 14 times in every block.
All inputs are finite; a program needn't handle non-finite values.
Results may differ from the reference program's by a relative error of at most 0.0003.
Values sent between devices are 32-bit elements; how exact they have to be, the bound alone decides.
No kernel may reach another device: no remote copies, remote signals or barrier semaphores. Data moves between devices by JAX's collectives and lax.ppermute only.
A program may use at most 128 MiB of HBM per device.

```python
import math
import jax
import jax.numpy as jnp
from jax import lax

NLEV = 72
CRM_Z = 50
CRM_X = 32
S_MAX = 4
PX = 8
PY = 128
COL_DEV = 1024
CAP = 14
SLOTS = 1792
NX = 128
NY = 1024
N_GX = 16
N_GY = 8


def draw_owner(key, part):
    key = jax.random.fold_in(key, 11)
    across = NX // PX
    along = NY // PY
    devices = SLOTS // CAP
    full_owner = jax.random.randint(jax.random.fold_in(key, 1), (), 0, devices)
    keys = jax.random.split(jax.random.fold_in(key, 2), across * along)

    def one(sub):
        first, second = jax.random.split(sub)
        scores = jax.random.randint(first, (SLOTS,), 1, 2 ** 18)
        slot_ids = jnp.arange(SLOTS, dtype=jnp.int32)
        scores = jnp.where(slot_ids // CAP == full_owner, 0, scores)
        order = jnp.argsort(scores * SLOTS + slot_ids, stable=True)
        chosen = order[:PX * PY] // CAP
        placed = jax.random.permutation(second, PX * PY)
        return chosen[placed].astype(jnp.int32)
    owners = jax.vmap(one)(keys)
    return owners.reshape(across, along, PX, PY).transpose(0, 2, 1, 3).reshape(NX, NY)


def draw_counts(key, part):
    key = jax.random.fold_in(key, 12)
    across = NX // PX
    along = NY // PY
    first, second = jax.random.split(key)
    region = jax.random.randint(first, (across, along, 1, 1), 1, S_MAX + 1)
    jitter = jax.random.randint(second, (across, along, PX, PY), -1, 2)
    steps_col = jnp.clip(region + jitter, 1, S_MAX)
    steps_col = steps_col.transpose(0, 2, 1, 3).reshape(NX, NY)
    return steps_col.at[0, 0].set(S_MAX).astype(jnp.int32)


def level_of(own_key, dims, shards, least, high):
    def one(dim, shards_of):
        draws = jax.random.uniform(jax.random.fold_in(jax.random.fold_in(own_key, 6), dim), (shards_of,), jnp.float32, least / len(shards), high / len(shards))
        return jnp.repeat(jnp.exp(draws), dims[dim] // shards_of).reshape((-1,) + (1,) * (len(dims) - dim - 1))

    gain = one(*shards[0])
    for cut in shards[1:]:
        gain = gain * one(*cut)
    return gain


def normal_values(stream_key, dims, width, bound, shards=(), kind=jnp.bfloat16):
    entries = jax.random.normal(stream_key, dims, jnp.float32) * width
    if len(shards) > 0:
        entries = level_of(stream_key, dims, shards, -0.22, 0.18) * entries
    return jnp.clip(entries, min=-bound, max=bound).astype(kind)


def setup_inputs(seed: int = 0) -> dict:
    streams_of = jax.random.split(jax.random.key(seed), 9)
    return {
        "state": normal_values(streams_of[0], (2 * NLEV, NX, NY), 1.0, 6.0, ((1, 16), (2, 8)), jnp.float32),
        "owner": draw_owner(jax.random.fold_in(streams_of[8], 71), 0),
        "counts": draw_counts(jax.random.fold_in(streams_of[8], 71), 0),
        "vert": normal_values(streams_of[3], (NLEV, NLEV), NLEV ** -0.5, 0.75, (), jnp.float32),
        "down_map": normal_values(streams_of[4], (CRM_Z, NLEV), NLEV ** -0.5, 0.75, (), jnp.float32),
        "up_map": normal_values(streams_of[5], (NLEV, CRM_Z), CRM_Z ** -0.5, 0.875, (), jnp.float32),
        "courant": jnp.clip(jnp.exp(jax.random.uniform(streams_of[6], (CRM_Z,), jnp.float32, math.log(0.05), math.log(0.9))), 0.05, 0.9),
        "crm_field": normal_values(streams_of[7], (2 * CRM_Z * CRM_X, SLOTS * N_GX * N_GY), 0.5, 4.0, ((1, 128),), jnp.float32),
    }


diffusion_rate = 0.1
condense_rate = 0.5
latent_heat = 1.0
moisture_slope = 0.3


def profiles(columns, down_map):
    levels = columns.reshape(2, down_map.shape[1], -1)
    return jnp.einsum("zl,vlb->vzb", down_map, levels, precision=lax.Precision.HIGHEST)


def advance(fields, courant, active):
    shifted = jnp.roll(fields, 1, axis=2)
    moved = fields - courant[None, :, None, None] * (fields - shifted)
    temper = moved[0]
    vapour = moved[1]
    condensed = condense_rate * jnp.maximum(vapour - jnp.exp(moisture_slope * temper), 0.0)
    result = jnp.stack([temper + latent_heat * condensed, vapour - condensed])
    return jnp.where(active[None, None, None, :], result, fields)


def tendency(init, steps_col, courant, up_map):
    def turn(step, fields):
        return advance(fields, courant, step < steps_col)

    final = lax.fori_loop(0, S_MAX, turn, init)
    change = jnp.mean(final - init, axis=2)
    out = jnp.einsum("lz,vzb->vlb", up_map, change, precision=lax.Precision.HIGHEST)
    return out.reshape(2 * up_map.shape[0], -1)


def reference(state, owner, counts, vert, down_map, up_map, courant, crm_field):
    lap = (jnp.roll(state, 1, 1) + jnp.roll(state, -1, 1) + jnp.roll(state, 1, 2)
           + jnp.roll(state, -1, 2) - 4.0 * state)
    levels = state.reshape(2, NLEV, NX, NY)
    mixed = jnp.einsum("ij,vjxy->vixy", vert, levels, precision=lax.Precision.HIGHEST)
    dyn = state + diffusion_rate * lap + mixed.reshape(state.shape)
    across = NX // PX
    along = NY // PY
    devices = across * along
    col_blocks = dyn.reshape(2 * NLEV, across, PX, along, PY).transpose(1, 3, 0, 2, 4).reshape(devices, 2 * NLEV, COL_DEV)
    own_blocks = owner.reshape(across, PX, along, PY).transpose(0, 2, 1, 3).reshape(devices, COL_DEV)
    step_blocks = counts.reshape(across, PX, along, PY).transpose(0, 2, 1, 3).reshape(devices, COL_DEV)
    sources = jnp.arange(devices, dtype=jnp.int32)
    owner_ids = jnp.arange(devices, dtype=jnp.int32)

    def one(inputs):
        block_cols, block_own, block_steps, source = inputs
        onehot = (block_own[:, None] == owner_ids[None, :]).astype(jnp.int32)
        ranks = jnp.sum(jnp.cumsum(onehot, axis=0) * onehot, axis=1) - 1
        index = (block_own * SLOTS + source * CAP + ranks).astype(jnp.int32)
        field = jnp.take(crm_field, index, axis=1).reshape(2, CRM_Z, CRM_X, COL_DEV)
        prof = profiles(block_cols, down_map)
        init = prof[:, :, None, :] + field
        return tendency(init, block_steps, courant, up_map)

    tends = lax.map(one, (col_blocks, own_blocks, step_blocks, sources))
    tend = tends.reshape(across, along, 2 * NLEV, PX, PY).transpose(2, 0, 3, 1, 4).reshape(2 * NLEV, NX, NY)
    return dyn + tend
```

```python
import functools
import math

import jax
import jax.numpy as jnp
from jax import lax
from jax.experimental import pallas as pl
from jax.experimental.pallas import tpu as pltpu
from jax.sharding import PartitionSpec as P

S_MAX = 4
DIFFUSION = 0.1
CONDENSE = 0.5
SLOPE = 0.3
LANES = 128
BETA = SLOPE * math.log2(math.e)
SHIFT = math.log2(BETA)

NT = (((1,), (1,)), ((), ()))
NN = (((1,), (0,)), ((), ()))
TN = (((0,), (0,)), ((), ()))


def split(value):
    high = value.astype(jnp.bfloat16)
    low = (value - high.astype(jnp.float32)).astype(jnp.bfloat16)
    return high, low


def dot(a, b, dims=NN):
    return lax.dot_general(a, b, dims, preferred_element_type=jnp.float32)


def dot3(a, b):
    a_hi, a_lo = split(a)
    b_hi, b_lo = split(b)
    return dot(a_hi, b_hi) + (dot(a_hi, b_lo) + dot(a_lo, b_hi))


def edges_kernel(state_ref, top_ref, bottom_ref, side_ref):
    levels = top_ref.shape[0]
    top_ref[...] = state_ref[pl.ds(0, levels, stride=8), :]
    bottom_ref[...] = state_ref[pl.ds(7, levels, stride=8), :]
    row = lax.broadcasted_iota(jnp.int32, (8, LANES), 0)
    lane = lax.broadcasted_iota(jnp.int32, (8, LANES), 1)
    pick = ((row == 0) & (lane == 0)) | ((row == 1) & (lane == LANES - 1))
    pick = pick.astype(jnp.bfloat16)
    data = state_ref[...]
    hi = data.astype(jnp.bfloat16)
    rest = data - hi.astype(jnp.float32)
    mid = rest.astype(jnp.bfloat16)
    low = (rest - mid.astype(jnp.float32)).astype(jnp.bfloat16)
    side_ref[...] = (dot(pick, hi, NT) + dot(pick, mid, NT)) + dot(pick, low, NT)


def columns_kernel(
    cap, state_ref, above_ref, below_ref, left_ref, right_ref, owner_ref, counts_ref,
    vert_ref, down_ref, dyn_ref, slot_ref, out_ref,
):
    levels = above_ref.shape[0]
    half = levels // 2
    crm_z = down_ref.shape[0]
    pad_z = -(-crm_z // 8) * 8
    lane = lax.broadcasted_iota(jnp.int32, (8, LANES), 1)
    row = lax.broadcasted_iota(jnp.int32, (8, LANES), 0)
    sides = jnp.concatenate([left_ref[...], right_ref[...], jnp.zeros((6, 8 * levels), jnp.float32)], axis=0)
    place = ((row == 0) & (lane == 0)) | ((row == 1) & (lane == LANES - 1))
    place = place.astype(jnp.bfloat16)
    s_hi, s_lo = split(sides)
    dyn_ref[...] = dot(s_hi, place, TN) + dot(s_lo, place, TN)
    wide = lax.broadcasted_iota(jnp.int32, (levels, LANES), 1)
    rows = [state_ref[pl.ds(i, levels, stride=8), :] for i in range(8)]
    laps = []
    for i in range(8):
        mid = rows[i]
        up = rows[i - 1] if i > 0 else above_ref[...]
        dn = rows[i + 1] if i < 7 else below_ref[...]
        west = jnp.where(wide == 0, 0.0, pltpu.roll(mid, 1, 1))
        east = jnp.where(wide == LANES - 1, 0.0, pltpu.roll(mid, LANES - 1, 1))
        halo = dyn_ref[pl.ds(i, levels, stride=8), :]
        lap = (up + dn + (west + east + halo)) - 4.0 * mid
        laps.append(mid + DIFFUSION * lap)
    whole = jnp.concatenate(rows, axis=1)
    base = jnp.concatenate(laps, axis=1)
    vert = vert_ref[...]
    temper = base[:half] + dot3(vert, whole[:half])
    vapour = base[half:] + dot3(vert, whole[half:])
    down = jnp.concatenate([down_ref[...], jnp.zeros((pad_z - crm_z, half), jnp.float32)], axis=0)
    prof_t = dot3(down, temper)
    prof_q = dot3(down, vapour)
    for i in range(8):
        cols = slice(i * LANES, (i + 1) * LANES)
        dyn_ref[pl.ds(i, half, stride=8), :] = temper[:, cols]
        dyn_ref[pl.ds(8 * half + i, half, stride=8), :] = vapour[:, cols]

    owner = jnp.concatenate([owner_ref[i:i + 1, :] for i in range(8)], axis=1)
    counts = jnp.concatenate([counts_ref[i:i + 1, :] for i in range(8)], axis=1)
    width = owner.shape[1]
    devices = out_ref.shape[0] // cap
    which = lax.broadcasted_iota(jnp.int32, (devices, width), 0)
    mine = which == owner
    earlier = (
        lax.broadcasted_iota(jnp.int32, (width, width), 0)
        < lax.broadcasted_iota(jnp.int32, (width, width), 1)
    ).astype(jnp.bfloat16)
    before = dot(mine.astype(jnp.bfloat16), earlier)
    rank = jnp.sum(jnp.where(mine, before, 0.0), axis=0, keepdims=True).astype(jnp.int32)
    slot = owner * cap + rank
    slot_ref[...] = slot

    lead = (lax.broadcasted_iota(jnp.int32, (8, width), 0) == 0).astype(jnp.float32)
    steps = lead * counts.astype(jnp.float32)
    blank = jnp.zeros((LANES - 2 * pad_z - 8, width), jnp.float32)
    payload = jnp.concatenate([prof_t, prof_q, steps, blank], axis=0)
    p_hi, p_lo = split(payload)
    both = jnp.concatenate([p_hi, p_lo], axis=0)
    chunk = 256
    for start in range(0, out_ref.shape[0], chunk):
        ids = start + lax.broadcasted_iota(jnp.int32, (chunk, width), 0)
        pick = (ids == slot).astype(jnp.bfloat16)
        sent = dot(pick, both, NT)
        out_ref[start:start + chunk, :] = sent[:, :LANES] + sent[:, LANES:]


def crm_kernel(crm_z, crm_x, courant_ref, arrived_ref, field_ref, out_ref, prof_ref, part_ref, turn_ref):
    pad_z = -(-crm_z // 8) * 8
    quads = crm_x // 8
    cols = arrived_ref[...].T
    prof_t = cols[:pad_z]
    prof_q = cols[pad_z:2 * pad_z]
    counts = cols[2 * pad_z:2 * pad_z + 1]
    prof_ref[:pad_z, :] = BETA * (prof_t + prof_q) + SHIFT
    prof_ref[pad_z:2 * pad_z, :] = BETA * prof_q
    on = [jnp.broadcast_to(counts > float(k), (8, LANES)) for k in range(1, S_MAX)]

    def level(z, carry):
        c = courant_ref[z]
        keep = 1.0 - c
        base_s = jnp.broadcast_to(prof_ref[pl.ds(z, 1), :], (8, LANES))
        base_q = jnp.broadcast_to(prof_ref[pl.ds(pad_z + z, 1), :], (8, LANES))
        temper = [field_ref[pl.ds(z * crm_x + i, 8, stride=quads), :] for i in range(quads)]
        vapour = [field_ref[pl.ds((crm_z + z) * crm_x + i, 8, stride=quads), :] for i in range(quads)]
        sums = [t + v for t, v in zip(temper, vapour)]

        def advect(values, stay, come):
            moved = [come * v for v in values]
            last = pltpu.roll(moved[-1], 1, 0)
            return [stay * v + m for v, m in zip(values, [last] + moved[:-1])]

        def total(values):
            while len(values) > 1:
                values = [a + b for a, b in zip(values[::2], values[1::2])]
            return values[0]

        sums = [s + base_s for s in advect(sums, BETA * keep, BETA * c)]
        vapour = [v + base_q for v in advect(vapour, BETA * keep, BETA * c)]
        gone = None
        for k in range(S_MAX):
            if k > 0:
                sums = advect(sums, keep, c)
                vapour = advect(vapour, 0.5 * keep, 0.5 * c)
            excess = [jnp.maximum(v - jnp.exp2(s - v), 0.0) for s, v in zip(sums, vapour)]
            lost = total(excess)
            gone = lost if k == 0 else gone + jnp.where(on[k - 1], lost, 0.0)
            if k < S_MAX - 1:
                vapour = [(v + v) - e for v, e in zip(vapour, excess)]
        part_ref[pl.ds(8 * z, 8), :] = gone
        return carry

    lax.fori_loop(0, crm_z, level, 0, unroll=2)
    scale = CONDENSE / (BETA * crm_x)
    part_ref[8 * crm_z:, :] = jnp.zeros((8 * (64 - crm_z), LANES), jnp.float32)
    change = part_ref[pl.ds(0, 64, stride=8), :]
    for i in range(1, 8):
        change = change + part_ref[pl.ds(i, 64, stride=8), :]
    change = change * scale
    turn_ref[...] = jnp.concatenate([change, change], axis=0).T
    lane = lax.broadcasted_iota(jnp.int32, (LANES // 2, LANES), 1)
    even = turn_ref[pl.ds(0, LANES // 2, stride=2), :]
    odd = turn_ref[pl.ds(1, LANES // 2, stride=2), :]
    out_ref[...] = jnp.where(lane < LANES // 2, even, odd)


def final_kernel(dyn_ref, returned_ref, slot_ref, up_ref, out_ref):
    half, crm_z = up_ref.shape
    slot = slot_ref[...]
    width = slot.shape[1]
    pairs = returned_ref.shape[0]
    r_hi, r_lo = split(returned_ref[...])
    both = jnp.concatenate([r_hi, r_lo], axis=1)
    ids = lax.broadcasted_iota(jnp.int32, (pairs, width), 0)
    pick = (ids == slot // 2).astype(jnp.bfloat16)
    got = dot(both, pick, TN)
    got = got[:LANES] + got[LANES:]
    change = jnp.where(slot % 2 == 0, got[:LANES // 2], got[LANES // 2:])
    up = jnp.concatenate([up_ref[...], jnp.zeros((half, LANES // 2 - crm_z), jnp.float32)], axis=1)
    tend = dot3(up, change)
    for i in range(8):
        cols = slice(i * LANES, (i + 1) * LANES)
        top = pl.ds(i, half, stride=8)
        bottom = pl.ds(8 * half + i, half, stride=8)
        out_ref[top, :] = dyn_ref[top, :] + tend[:, cols]
        out_ref[bottom, :] = dyn_ref[bottom, :] - tend[:, cols]


VMEM = pl.BlockSpec(memory_space=pltpu.VMEM)


def params(limit_mib=40):
    return pltpu.CompilerParams(vmem_limit_bytes=limit_mib * 2**20)


def crm(courant, arrived, crm_field, crm_z, crm_x, interpret=False):
    slots = arrived.shape[0]
    rows = crm_field.shape[0]
    pad_z = -(-crm_z // 8) * 8
    return pl.pallas_call(
        functools.partial(crm_kernel, crm_z, crm_x),
        grid=(slots // LANES,),
        in_specs=[
            pl.BlockSpec(memory_space=pltpu.SMEM),
            pl.BlockSpec((LANES, LANES), lambda b: (b, 0)),
            pl.BlockSpec((rows, LANES), lambda b: (0, b)),
        ],
        out_specs=pl.BlockSpec((LANES // 2, LANES), lambda b: (b, 0)),
        out_shape=jax.ShapeDtypeStruct((slots // 2, LANES), jnp.float32),
        scratch_shapes=[
            pltpu.VMEM((2 * pad_z, LANES), jnp.float32),
            pltpu.VMEM((8 * 64, LANES), jnp.float32),
            pltpu.VMEM((LANES, LANES), jnp.float32),
        ],
        compiler_params=params(),
        name="crm",
    )(courant, arrived, crm_field)


def body(state, owner, counts, vert, down_map, up_map, courant, crm_field):
    rows, width_x, width_y = state.shape
    col_dev = width_x * width_y
    across = lax.axis_size("gx")
    along = lax.axis_size("gy")
    devices = across * along
    cap = max(2, 7 * col_dev // (4 * devices))
    slots = devices * cap
    crm_z = down_map.shape[0]
    crm_x = crm_field.shape[0] // (2 * crm_z)
    flat = state.reshape(rows * width_x, width_y)

    f32 = lambda *shape: jax.ShapeDtypeStruct(shape, jnp.float32)
    top, bottom, side = pl.pallas_call(
        edges_kernel,
        in_specs=[VMEM],
        out_specs=[VMEM] * 3,
        out_shape=[f32(rows, width_y), f32(rows, width_y), f32(8, rows * width_x)],
        compiler_params=params(),
        name="edges",
    )(flat)

    def shifted(value, axis, step):
        count = lax.axis_size(axis)
        return lax.ppermute(value, axis, [(i, (i + step) % count) for i in range(count)])

    above = shifted(bottom, "gx", 1)
    below = shifted(top, "gx", -1)
    left = shifted(side[1:2], "gy", 1)
    right = shifted(side[0:1], "gy", -1)

    dyn, slot, outgoing = pl.pallas_call(
        functools.partial(columns_kernel, cap),
        in_specs=[VMEM] * 9,
        out_specs=[VMEM] * 3,
        out_shape=[
            f32(rows * width_x, width_y),
            jax.ShapeDtypeStruct((1, col_dev), jnp.int32),
            f32(slots, LANES),
        ],
        compiler_params=params(),
        name="columns",
    )(flat, above, below, left, right, owner, counts, vert, down_map)

    arrived = lax.all_to_all(outgoing, ("gx", "gy"), split_axis=0, concat_axis=0, tiled=True)
    change = crm(courant, arrived, crm_field, crm_z, crm_x)
    returned = lax.all_to_all(change, ("gx", "gy"), split_axis=0, concat_axis=0, tiled=True)

    out = pl.pallas_call(
        final_kernel,
        in_specs=[VMEM] * 4,
        out_specs=VMEM,
        out_shape=f32(rows * width_x, width_y),
        compiler_params=params(),
        name="final",
    )(dyn, returned, slot, up_map)
    return out.reshape(state.shape)


def solution(mesh):
    in_specs = (
        P(None, "gx", "gy"),
        P("gx", "gy"),
        P("gx", "gy"),
        P(),
        P(),
        P(),
        P(),
        P(None, ("gx", "gy")),
    )
    out_specs = P(None, "gx", "gy")
    return jax.shard_map(body, mesh=mesh, in_specs=in_specs, out_specs=out_specs, check_vma=False)
```

```python
import functools
import math

import jax
import jax.numpy as jnp
from jax import lax
from jax.experimental import pallas as pl
from jax.experimental.pallas import tpu as pltpu
from jax.sharding import PartitionSpec as P

S_MAX = 4
DIFFUSION = 0.1
CONDENSE = 0.5
SLOPE = 0.3
LANES = 128
SUBL = 8
BETA = SLOPE * math.log2(math.e)
SHIFT = math.log2(BETA)

NT = (((1,), (1,)), ((), ()))
NN = (((1,), (0,)), ((), ()))
TN = (((0,), (0,)), ((), ()))


def split(value):
    high = value.astype(jnp.bfloat16)
    low = (value - high.astype(jnp.float32)).astype(jnp.bfloat16)
    return high, low


def dot(a, b, dims=NN):
    return lax.dot_general(a, b, dims, preferred_element_type=jnp.float32)


def dot3(a, b):
    a_hi, a_lo = split(a)
    b_hi, b_lo = split(b)
    return dot(a_hi, b_hi) + (dot(a_hi, b_lo) + dot(a_lo, b_hi))


def edges_kernel(state_ref, top_ref, bottom_ref, west_ref, east_ref):
    levels = top_ref.shape[0]
    rows = [state_ref[pl.ds(i, levels, stride=SUBL), :] for i in range(SUBL)]
    top_ref[...] = rows[0]
    bottom_ref[...] = rows[-1]
    row = lax.broadcasted_iota(jnp.int32, (SUBL, LANES), 0)
    lane = lax.broadcasted_iota(jnp.int32, (SUBL, LANES), 1)
    pick = ((row == 0) & (lane == 0)) | ((row == 1) & (lane == LANES - 1))
    pick = pick.astype(jnp.bfloat16)
    for i in range(SUBL):
        hi, lo = split(rows[i])
        side = dot(pick, hi, NT) + dot(pick, lo, NT)
        west_ref[i:i + 1, :] = side[0:1]
        east_ref[i:i + 1, :] = side[1:2]


def local_kernel(
    cap, state_ref, owner_hbm, counts_hbm, vert_hbm, courant_hbm, down_hbm,
    base_ref, slot_ref, steps_ref, const_ref, down_ref,
    owner_ref, counts_ref, vert_ref, courant_ref, sems,
):
    copies = [
        pltpu.make_async_copy(src, dst, sems.at[i])
        for i, (src, dst) in enumerate(
            [
                (owner_hbm, owner_ref),
                (counts_hbm, counts_ref),
                (vert_hbm, vert_ref),
                (courant_hbm, courant_ref),
                (down_hbm, down_ref),
            ]
        )
    ]
    for copy in copies:
        copy.start()
    levels = base_ref.shape[0]
    half = levels // 2
    crm_z = courant_ref.shape[0]
    wide = lax.broadcasted_iota(jnp.int32, (levels, LANES), 1)
    rows = [state_ref[pl.ds(i, levels, stride=SUBL), :] for i in range(SUBL)]
    laps = []
    for i in range(SUBL):
        mid = rows[i]
        lap = jnp.where(wide == 0, 0.0, pltpu.roll(mid, 1, 1))
        lap = lap + jnp.where(wide == LANES - 1, 0.0, pltpu.roll(mid, LANES - 1, 1))
        if i > 0:
            lap = lap + rows[i - 1]
        if i < SUBL - 1:
            lap = lap + rows[i + 1]
        laps.append(mid + DIFFUSION * (lap - 4.0 * mid))
    whole = jnp.concatenate(rows, axis=1)
    base = jnp.concatenate(laps, axis=1)
    copies[2].wait()
    vert = vert_ref[...]
    base_ref[:half, :] = base[:half] + dot3(vert, whole[:half])
    base_ref[half:, :] = base[half:] + dot3(vert, whole[half:])

    copies[0].wait()
    owner = jnp.concatenate([owner_ref[i:i + 1, :] for i in range(SUBL)], axis=1)
    width = owner.shape[1]
    devices = LANES * (-(-DEVICES // LANES))
    mine = lax.broadcasted_iota(jnp.int32, (devices, width), 0) == owner
    earlier = (
        lax.broadcasted_iota(jnp.int32, (width, width), 0)
        < lax.broadcasted_iota(jnp.int32, (width, width), 1)
    ).astype(jnp.bfloat16)
    before = dot(mine.astype(jnp.bfloat16), earlier)
    rank = jnp.sum(jnp.where(mine, before, 0.0), axis=0, keepdims=True).astype(jnp.int32)
    slot_ref[...] = owner * cap + rank
    copies[1].wait()
    counts = jnp.concatenate([counts_ref[i:i + 1, :] for i in range(SUBL)], axis=1)
    lead = (lax.broadcasted_iota(jnp.int32, (SUBL, width), 0) == 0).astype(jnp.float32)
    steps_ref[...] = lead * counts.astype(jnp.float32)
    copies[3].wait()
    row = lax.broadcasted_iota(jnp.int32, (SUBL, LANES), 0)
    for z in range(crm_z):
        c = courant_ref[z]
        keep = 1.0 - c
        part = jnp.where(row % 2 == 0, keep, c)
        const_ref[SUBL * z:SUBL * (z + 1), :] = part * jnp.where(row < 2, BETA, jnp.where(row < 4, 1.0, 0.5))
    copies[4].wait()


def send_kernel(
    base_ref, slot_ref, steps_ref, down_ref, above_ref, below_ref, left_ref, right_ref,
    dyn_ref, out_ref,
):
    levels, width = base_ref.shape
    half = levels // 2
    crm_z = down_ref.shape[0]
    pad_z = -(-crm_z // SUBL) * SUBL
    sides = jnp.concatenate([left_ref[...], right_ref[...]], axis=0)
    row = lax.broadcasted_iota(jnp.int32, (2 * SUBL, width), 0)
    lane = lax.broadcasted_iota(jnp.int32, (2 * SUBL, width), 1)
    target = jnp.where(row < SUBL, row * LANES, (row - SUBL) * LANES + (LANES - 1))
    place = (lane == target).astype(jnp.bfloat16)
    s_hi, s_lo = split(sides)
    halo = dot(s_hi, place, TN) + dot(s_lo, place, TN)
    first = halo[:, :LANES] + above_ref[...]
    last = halo[:, width - LANES:] + below_ref[...]
    halo = jnp.concatenate([first, halo[:, LANES:width - LANES], last], axis=1)
    dyn = base_ref[...] + DIFFUSION * halo
    dyn_ref[...] = dyn
    down = jnp.concatenate([down_ref[...], jnp.zeros((pad_z - crm_z, half), jnp.float32)], axis=0)
    prof_t = dot3(down, dyn[:half])
    prof_q = dot3(down, dyn[half:])
    blank = jnp.zeros((LANES - 2 * pad_z - SUBL, width), jnp.float32)
    payload = jnp.concatenate([prof_t, prof_q, steps_ref[...], blank], axis=0)
    p_hi, p_lo = split(payload)
    both = jnp.concatenate([p_hi, p_lo], axis=0)
    slot = slot_ref[...]
    chunk = 256
    for start in range(0, out_ref.shape[0], chunk):
        ids = start + lax.broadcasted_iota(jnp.int32, (chunk, width), 0)
        sent = dot((ids == slot).astype(jnp.bfloat16), both, NT)
        out_ref[start:start + chunk, :] = sent[:, :LANES] + sent[:, LANES:]


def total(values):
    while len(values) > 1:
        values = [a + b for a, b in zip(values[::2], values[1::2])]
    return values[0]


def advect(values, stay, come):
    moved = [come * v for v in values]
    last = pltpu.roll(moved[-1], 1, 0)
    return [stay * v + m for v, m in zip(values, [last] + moved[:-1])]


def crm_kernel(crm_z, crm_x, const_ref, arrived_ref, field_ref, out_ref, prof_ref, part_ref, turn_ref):
    pad_z = -(-crm_z // SUBL) * SUBL
    quads = crm_x // SUBL
    cols = arrived_ref[...].T
    prof_ref[:pad_z, :] = BETA * cols[:pad_z] + SHIFT
    prof_ref[pad_z:2 * pad_z, :] = BETA * cols[pad_z:2 * pad_z]
    counts = jnp.broadcast_to(cols[2 * pad_z:2 * pad_z + 1], (SUBL, LANES))
    part = jnp.where(counts > 3.0, 0.0625, jnp.where(counts > 2.0, 0.125, jnp.where(counts > 1.0, 0.25, 0.5)))
    scale = 2.0 * CONDENSE / (BETA * crm_x)
    w_first = (1.0 - part) * scale
    w_kept = [jnp.where(counts > float(k), part * (-scale * 2.0**k), 0.0) for k in range(S_MAX)]

    def spread(ref, row):
        return jnp.broadcast_to(ref[pl.ds(row, 1), :], (SUBL, LANES))

    for z in range(crm_z):
        beta_keep, beta_c, keep, c, half_keep, half_c = [spread(const_ref, SUBL * z + i) for i in range(6)]
        base_t = spread(prof_ref, z)
        base_q = spread(prof_ref, pad_z + z)
        temper = [field_ref[pl.ds(z * crm_x + i, SUBL, stride=quads), :] for i in range(quads)]
        vapour = [field_ref[pl.ds((crm_z + z) * crm_x + i, SUBL, stride=quads), :] for i in range(quads)]
        temper = [t + base_t for t in advect(temper, beta_keep, beta_c)]
        vapour = [v + base_q for v in advect(vapour, beta_keep, beta_c)]
        sums = [t + v for t, v in zip(temper, vapour)]
        gone = w_first * total(vapour)
        for k in range(S_MAX):
            if k > 0:
                sums = advect(sums, keep, c)
                vapour = advect(vapour, half_keep, half_c)
                temper = [s - v for s, v in zip(sums, vapour)]
            kept = [jnp.minimum(v, jnp.exp2(t)) for t, v in zip(temper, vapour)]
            gone = gone + w_kept[k] * total(kept)
            if k < S_MAX - 1:
                vapour = [v + e for v, e in zip(vapour, kept)]
        part_ref[SUBL * z:SUBL * (z + 1), :] = gone
    part_ref[SUBL * crm_z:, :] = jnp.zeros((SUBL * (LANES // 2 - crm_z), LANES), jnp.float32)
    change = part_ref[pl.ds(0, LANES // 2, stride=SUBL), :]
    for i in range(1, SUBL):
        change = change + part_ref[pl.ds(i, LANES // 2, stride=SUBL), :]
    turn_ref[...] = jnp.concatenate([change, change], axis=0).T
    lane = lax.broadcasted_iota(jnp.int32, (LANES // 2, LANES), 1)
    even = turn_ref[pl.ds(0, LANES // 2, stride=2), :]
    odd = turn_ref[pl.ds(1, LANES // 2, stride=2), :]
    out_ref[...] = jnp.where(lane < LANES // 2, even, odd)


def final_kernel(dyn_ref, returned_ref, slot_ref, up_ref, out_ref):
    half, crm_z = up_ref.shape
    slot = slot_ref[...]
    width = slot.shape[1]
    pairs = returned_ref.shape[0]
    r_hi, r_lo = split(returned_ref[...])
    both = jnp.concatenate([r_hi, r_lo], axis=1)
    ids = lax.broadcasted_iota(jnp.int32, (pairs, width), 0)
    pick = (ids == slot // 2).astype(jnp.bfloat16)
    got = dot(both, pick, TN)
    got = got[:LANES] + got[LANES:]
    change = jnp.where(slot % 2 == 0, got[:LANES // 2], got[LANES // 2:])
    up = jnp.concatenate([up_ref[...], jnp.zeros((half, LANES // 2 - crm_z), jnp.float32)], axis=1)
    tend = dot3(up, change)
    for i in range(SUBL):
        cols = slice(i * LANES, (i + 1) * LANES)
        out_ref[pl.ds(i, half, stride=SUBL), :] = dyn_ref[:half, cols] + tend[:, cols]
        out_ref[pl.ds(SUBL * half + i, half, stride=SUBL), :] = dyn_ref[half:, cols] - tend[:, cols]


VMEM = pl.BlockSpec(memory_space=pltpu.VMEM)
HBM = pl.BlockSpec(memory_space=pltpu.HBM)
DEVICES = 128


def params(limit_mib=16):
    return pltpu.CompilerParams(vmem_limit_bytes=limit_mib * 2**20)


def f32(*shape):
    return jax.ShapeDtypeStruct(shape, jnp.float32)


def i32(*shape):
    return jax.ShapeDtypeStruct(shape, jnp.int32)


def crm(const, arrived, crm_field, crm_z, crm_x):
    slots = arrived.shape[0]
    rows = crm_field.shape[0]
    pad_z = -(-crm_z // SUBL) * SUBL
    return pl.pallas_call(
        functools.partial(crm_kernel, crm_z, crm_x),
        grid=(slots // LANES,),
        in_specs=[
            VMEM,
            pl.BlockSpec((LANES, LANES), lambda b: (b, 0)),
            pl.BlockSpec((rows, LANES), lambda b: (0, b)),
        ],
        out_specs=pl.BlockSpec((LANES // 2, LANES), lambda b: (b, 0)),
        out_shape=f32(slots // 2, LANES),
        scratch_shapes=[
            pltpu.VMEM((2 * pad_z, LANES), jnp.float32),
            pltpu.VMEM((SUBL * LANES // 2, LANES), jnp.float32),
            pltpu.VMEM((LANES, LANES), jnp.float32),
        ],
        compiler_params=params(48),
        name="crm",
    )(const, arrived, crm_field)


def exchange(value, devices):
    sent = value.reshape(devices, 1, -1)
    got = lax.all_to_all(sent, ("gx", "gy"), split_axis=0, concat_axis=0, tiled=True)
    return got.reshape(value.shape)


def shifted(value, axis, step):
    count = lax.axis_size(axis)
    return lax.ppermute(value, axis, [(i, (i + step) % count) for i in range(count)])


def body(state, owner, counts, vert, down_map, up_map, courant, crm_field):
    rows, width_x, width_y = state.shape
    col_dev = width_x * width_y
    devices = lax.axis_size("gx") * lax.axis_size("gy")
    cap = max(2, 7 * col_dev // (4 * devices))
    slots = devices * cap
    crm_z = down_map.shape[0]
    crm_x = crm_field.shape[0] // (2 * crm_z)
    flat = state.reshape(rows * width_x, width_y)

    top, bottom, west, east = pl.pallas_call(
        edges_kernel,
        in_specs=[VMEM],
        out_specs=[VMEM] * 4,
        out_shape=[f32(rows, width_y), f32(rows, width_y), f32(width_x, rows), f32(width_x, rows)],
        compiler_params=params(),
        name="edges",
    )(flat)

    above = shifted(bottom, "gx", 1)
    below = shifted(top, "gx", -1)
    left = shifted(east, "gy", 1)
    right = shifted(west, "gy", -1)

    base, slot, steps, const, down = pl.pallas_call(
        functools.partial(local_kernel, cap),
        in_specs=[VMEM] + [HBM] * 5,
        out_specs=[VMEM] * 5,
        out_shape=[f32(rows, col_dev), i32(1, col_dev), f32(SUBL, col_dev), f32(SUBL * crm_z, LANES), f32(*down_map.shape)],
        scratch_shapes=[
            pltpu.VMEM(owner.shape, jnp.int32),
            pltpu.VMEM(counts.shape, jnp.int32),
            pltpu.VMEM(vert.shape, jnp.float32),
            pltpu.SMEM(courant.shape, jnp.float32),
            pltpu.SemaphoreType.DMA((5,)),
        ],
        compiler_params=params(),
        cost_estimate=pl.CostEstimate(flops=10**9, bytes_accessed=4 * 10**6, transcendentals=0),
        name="local",
    )(flat, owner, counts, vert, courant, down_map)

    dyn, outgoing = pl.pallas_call(
        send_kernel,
        in_specs=[VMEM] * 8,
        out_specs=[VMEM] * 2,
        out_shape=[f32(rows, col_dev), f32(slots, LANES)],
        compiler_params=params(),
        name="send",
    )(base, slot, steps, down, above, below, left, right)

    arrived = exchange(outgoing, devices)
    change = crm(const, arrived, crm_field, crm_z, crm_x)
    returned = exchange(change, devices)

    out = pl.pallas_call(
        final_kernel,
        in_specs=[VMEM] * 4,
        out_specs=VMEM,
        out_shape=f32(rows * width_x, width_y),
        compiler_params=params(),
        name="final",
    )(dyn, returned, slot, up_map)
    return out.reshape(state.shape)


def solution(mesh):
    in_specs = (
        P(None, "gx", "gy"),
        P("gx", "gy"),
        P("gx", "gy"),
        P(),
        P(),
        P(),
        P(),
        P(None, ("gx", "gy")),
    )
    out_specs = P(None, "gx", "gy")
    return jax.shard_map(body, mesh=mesh, in_specs=in_specs, out_specs=out_specs, check_vma=False)
```

```python
import functools
import math

import jax
import jax.numpy as jnp
from jax import lax
from jax.experimental import pallas as pl
from jax.experimental.pallas import tpu as pltpu
from jax.sharding import PartitionSpec as P

S_MAX = 4
DIFFUSION = 0.1
CONDENSE = 0.5
SLOPE = 0.3
LANES = 128
SUBL = 8
BETA = SLOPE * math.log2(math.e)
SHIFT = math.log2(BETA)

NT = (((1,), (1,)), ((), ()))
NN = (((1,), (0,)), ((), ()))
TN = (((0,), (0,)), ((), ()))


def split(value):
    high = value.astype(jnp.bfloat16)
    low = (value - high.astype(jnp.float32)).astype(jnp.bfloat16)
    return high, low


def dot(a, b, dims=NN):
    return lax.dot_general(a, b, dims, preferred_element_type=jnp.float32)


def dot3(a, b):
    a_hi, a_lo = split(a)
    b_hi, b_lo = split(b)
    return dot(a_hi, b_hi) + (dot(a_hi, b_lo) + dot(a_lo, b_hi))


def edges_kernel(state_ref, top_ref, bottom_ref, west_ref, east_ref):
    levels = top_ref.shape[0]
    rows = [state_ref[pl.ds(i, levels, stride=SUBL), :] for i in range(SUBL)]
    top_ref[...] = rows[0]
    bottom_ref[...] = rows[-1]
    row = lax.broadcasted_iota(jnp.int32, (SUBL, LANES), 0)
    lane = lax.broadcasted_iota(jnp.int32, (SUBL, LANES), 1)
    pick = ((row == 0) & (lane == 0)) | ((row == 1) & (lane == LANES - 1))
    pick = pick.astype(jnp.bfloat16)
    for i in range(SUBL):
        hi, lo = split(rows[i])
        side = dot(pick, hi, NT) + dot(pick, lo, NT)
        west_ref[i:i + 1, :] = side[0:1]
        east_ref[i:i + 1, :] = side[1:2]


def local_kernel(cap, crm_z, state_ref, maps_ref, columns_ref, base_ref, slot_ref, steps_ref, const_ref):
    levels = base_ref.shape[0]
    half = levels // 2
    vert = maps_ref[:half, :half]
    columns = columns_ref[...]
    wide = lax.broadcasted_iota(jnp.int32, (levels, LANES), 1)
    rows = [state_ref[pl.ds(i, levels, stride=SUBL), :] for i in range(SUBL)]
    laps = []
    for i in range(SUBL):
        mid = rows[i]
        lap = jnp.where(wide == 0, 0.0, pltpu.roll(mid, 1, 1))
        lap = lap + jnp.where(wide == LANES - 1, 0.0, pltpu.roll(mid, LANES - 1, 1))
        if i > 0:
            lap = lap + rows[i - 1]
        if i < SUBL - 1:
            lap = lap + rows[i + 1]
        laps.append(mid + DIFFUSION * (lap - 4.0 * mid))
    whole = jnp.concatenate(rows, axis=1)
    base = jnp.concatenate(laps, axis=1)
    base_ref[:half, :] = base[:half] + dot3(vert, whole[:half])
    base_ref[half:, :] = base[half:] + dot3(vert, whole[half:])

    owner = jnp.concatenate([columns[i:i + 1, :] for i in range(SUBL)], axis=1)
    width = owner.shape[1]
    devices = LANES * (-(-DEVICES // LANES))
    mine = lax.broadcasted_iota(jnp.int32, (devices, width), 0) == owner
    earlier = (
        lax.broadcasted_iota(jnp.int32, (width, width), 0)
        < lax.broadcasted_iota(jnp.int32, (width, width), 1)
    ).astype(jnp.bfloat16)
    before = dot(mine.astype(jnp.bfloat16), earlier)
    rank = jnp.sum(jnp.where(mine, before, 0.0), axis=0, keepdims=True).astype(jnp.int32)
    slot_ref[...] = owner * cap + rank
    counts = jnp.concatenate([columns[i:i + 1, :] for i in range(SUBL, 2 * SUBL)], axis=1)
    lead = (lax.broadcasted_iota(jnp.int32, (SUBL, width), 0) == 0).astype(jnp.float32)
    steps_ref[...] = lead * counts.astype(jnp.float32)
    last = maps_ref.shape[0] - SUBL
    line = jnp.broadcast_to(maps_ref[last:last + 1, :], (LANES, LANES))
    c = line.T[:crm_z]
    keep = 1.0 - c
    for i, value in enumerate((BETA * keep, BETA * c, keep, c, 0.5 * keep, 0.5 * c)):
        const_ref[pl.ds(i, crm_z, stride=SUBL), :] = value


def send_kernel(
    crm_z, base_ref, slot_ref, steps_ref, maps_ref, above_ref, below_ref, left_ref, right_ref,
    dyn_ref, out_ref,
):
    levels, width = base_ref.shape
    half = levels // 2
    pad_z = -(-crm_z // SUBL) * SUBL
    start = maps_ref.shape[0] - SUBL - pad_z
    down = maps_ref[start:start + pad_z, :half]
    sides = jnp.concatenate([left_ref[...], right_ref[...]], axis=0)
    row = lax.broadcasted_iota(jnp.int32, (2 * SUBL, width), 0)
    lane = lax.broadcasted_iota(jnp.int32, (2 * SUBL, width), 1)
    target = jnp.where(row < SUBL, row * LANES, (row - SUBL) * LANES + (LANES - 1))
    place = (lane == target).astype(jnp.bfloat16)
    s_hi, s_lo = split(sides)
    halo = dot(s_hi, place, TN) + dot(s_lo, place, TN)
    first = halo[:, :LANES] + above_ref[...]
    last = halo[:, width - LANES:] + below_ref[...]
    halo = jnp.concatenate([first, halo[:, LANES:width - LANES], last], axis=1)
    dyn = base_ref[...] + DIFFUSION * halo
    dyn_ref[...] = dyn
    prof_t = dot3(down, dyn[:half])
    prof_q = dot3(down, dyn[half:])
    blank = jnp.zeros((LANES - 2 * pad_z - SUBL, width), jnp.float32)
    payload = jnp.concatenate([prof_t, prof_q, steps_ref[...], blank], axis=0)
    p_hi, p_lo = split(payload)
    both = jnp.concatenate([p_hi, p_lo], axis=0)
    slot = slot_ref[...]
    chunk = 256
    for start in range(0, out_ref.shape[0], chunk):
        ids = start + lax.broadcasted_iota(jnp.int32, (chunk, width), 0)
        sent = dot((ids == slot).astype(jnp.bfloat16), both, NT)
        out_ref[start:start + chunk, :] = sent[:, :LANES] + sent[:, LANES:]


def total(values):
    while len(values) > 1:
        values = [a + b for a, b in zip(values[::2], values[1::2])]
    return values[0]


def advect(values, stay, come):
    moved = [come * v for v in values]
    last = pltpu.roll(moved[-1], 1, 0)
    return [stay * v + m for v, m in zip(values, [last] + moved[:-1])]


def crm_kernel(crm_z, crm_x, const_ref, arrived_ref, field_ref, out_ref, prof_ref, part_ref, turn_ref):
    pad_z = -(-crm_z // SUBL) * SUBL
    quads = crm_x // SUBL
    cols = arrived_ref[...].T
    prof_ref[:pad_z, :] = BETA * cols[:pad_z] + SHIFT
    prof_ref[pad_z:2 * pad_z, :] = BETA * cols[pad_z:2 * pad_z]
    counts = jnp.broadcast_to(cols[2 * pad_z:2 * pad_z + 1], (SUBL, LANES))
    part = jnp.where(counts > 3.0, 0.0625, jnp.where(counts > 2.0, 0.125, jnp.where(counts > 1.0, 0.25, 0.5)))
    scale = 2.0 * CONDENSE / (BETA * crm_x)
    w_first = (1.0 - part) * scale
    w_kept = [jnp.where(counts > float(k), part * (-scale * 2.0**k), 0.0) for k in range(S_MAX)]

    def spread(ref, row):
        return jnp.broadcast_to(ref[pl.ds(row, 1), :], (SUBL, LANES))

    for z in range(crm_z):
        beta_keep, beta_c, keep, c, half_keep, half_c = [spread(const_ref, SUBL * z + i) for i in range(6)]
        base_t = spread(prof_ref, z)
        base_q = spread(prof_ref, pad_z + z)
        temper = [field_ref[pl.ds(z * crm_x + i, SUBL, stride=quads), :] for i in range(quads)]
        vapour = [field_ref[pl.ds((crm_z + z) * crm_x + i, SUBL, stride=quads), :] for i in range(quads)]
        temper = [t + base_t for t in advect(temper, beta_keep, beta_c)]
        vapour = [v + base_q for v in advect(vapour, beta_keep, beta_c)]
        sums = [t + v for t, v in zip(temper, vapour)]
        gone = w_first * total(vapour)
        for k in range(S_MAX):
            if k > 0:
                sums = advect(sums, keep, c)
                vapour = advect(vapour, half_keep, half_c)
                temper = [s - v for s, v in zip(sums, vapour)]
            kept = [jnp.minimum(v, jnp.exp2(t)) for t, v in zip(temper, vapour)]
            gone = gone + w_kept[k] * total(kept)
            if k < S_MAX - 1:
                vapour = [v + e for v, e in zip(vapour, kept)]
        part_ref[SUBL * z:SUBL * (z + 1), :] = gone
    part_ref[SUBL * crm_z:, :] = jnp.zeros((SUBL * (LANES // 2 - crm_z), LANES), jnp.float32)
    change = part_ref[pl.ds(0, LANES // 2, stride=SUBL), :]
    for i in range(1, SUBL):
        change = change + part_ref[pl.ds(i, LANES // 2, stride=SUBL), :]
    turn_ref[...] = jnp.concatenate([change, change], axis=0).T
    lane = lax.broadcasted_iota(jnp.int32, (LANES // 2, LANES), 1)
    even = turn_ref[pl.ds(0, LANES // 2, stride=2), :]
    odd = turn_ref[pl.ds(1, LANES // 2, stride=2), :]
    out_ref[...] = jnp.where(lane < LANES // 2, even, odd)


def final_kernel(dyn_ref, returned_ref, slot_ref, up_ref, out_ref):
    half, crm_z = up_ref.shape
    slot = slot_ref[...]
    width = slot.shape[1]
    pairs = returned_ref.shape[0]
    r_hi, r_lo = split(returned_ref[...])
    both = jnp.concatenate([r_hi, r_lo], axis=1)
    ids = lax.broadcasted_iota(jnp.int32, (pairs, width), 0)
    pick = (ids == slot // 2).astype(jnp.bfloat16)
    got = dot(both, pick, TN)
    got = got[:LANES] + got[LANES:]
    change = jnp.where(slot % 2 == 0, got[:LANES // 2], got[LANES // 2:])
    up = jnp.concatenate([up_ref[...], jnp.zeros((half, LANES // 2 - crm_z), jnp.float32)], axis=1)
    tend = dot3(up, change)
    for i in range(SUBL):
        cols = slice(i * LANES, (i + 1) * LANES)
        out_ref[pl.ds(i, half, stride=SUBL), :] = dyn_ref[:half, cols] + tend[:, cols]
        out_ref[pl.ds(SUBL * half + i, half, stride=SUBL), :] = dyn_ref[half:, cols] - tend[:, cols]


VMEM = pl.BlockSpec(memory_space=pltpu.VMEM)
DEVICES = 128


def params(limit_mib=16):
    return pltpu.CompilerParams(vmem_limit_bytes=limit_mib * 2**20)


def f32(*shape):
    return jax.ShapeDtypeStruct(shape, jnp.float32)


def i32(*shape):
    return jax.ShapeDtypeStruct(shape, jnp.int32)


def crm(const, arrived, crm_field, crm_z, crm_x):
    slots = arrived.shape[0]
    rows = crm_field.shape[0]
    pad_z = -(-crm_z // SUBL) * SUBL
    return pl.pallas_call(
        functools.partial(crm_kernel, crm_z, crm_x),
        grid=(slots // LANES,),
        in_specs=[
            VMEM,
            pl.BlockSpec((LANES, LANES), lambda b: (b, 0)),
            pl.BlockSpec((rows, LANES), lambda b: (0, b)),
        ],
        out_specs=pl.BlockSpec((LANES // 2, LANES), lambda b: (b, 0)),
        out_shape=f32(slots // 2, LANES),
        scratch_shapes=[
            pltpu.VMEM((2 * pad_z, LANES), jnp.float32),
            pltpu.VMEM((SUBL * LANES // 2, LANES), jnp.float32),
            pltpu.VMEM((LANES, LANES), jnp.float32),
        ],
        compiler_params=params(48),
        name="crm",
    )(const, arrived, crm_field)


def exchange(value, devices):
    sent = value.reshape(devices, 1, -1)
    got = lax.all_to_all(sent, ("gx", "gy"), split_axis=0, concat_axis=0, tiled=True)
    return got.reshape(value.shape)


def stacked(values):
    tall = [-(-value.shape[0] // SUBL) * SUBL for value in values]
    parts, above = [], 0
    for value, height in zip(values, tall):
        below = sum(tall) - above - value.shape[0]
        parts.append(jnp.pad(value, ((above, below), (0, LANES - value.shape[1]))))
        above += height
    return sum(parts[1:], parts[0])


def shifted(value, axis, step):
    count = lax.axis_size(axis)
    return lax.ppermute(value, axis, [(i, (i + step) % count) for i in range(count)])


def body(state, owner, counts, vert, down_map, up_map, courant, crm_field):
    rows, width_x, width_y = state.shape
    col_dev = width_x * width_y
    devices = lax.axis_size("gx") * lax.axis_size("gy")
    cap = max(2, 7 * col_dev // (4 * devices))
    slots = devices * cap
    crm_z = down_map.shape[0]
    crm_x = crm_field.shape[0] // (2 * crm_z)
    flat = state.reshape(rows * width_x, width_y)

    top, bottom, west, east = pl.pallas_call(
        edges_kernel,
        in_specs=[VMEM],
        out_specs=[VMEM] * 4,
        out_shape=[f32(rows, width_y), f32(rows, width_y), f32(width_x, rows), f32(width_x, rows)],
        compiler_params=params(),
        name="edges",
    )(flat)

    above = shifted(bottom, "gx", 1)
    below = shifted(top, "gx", -1)
    left = shifted(east, "gy", 1)
    right = shifted(west, "gy", -1)

    maps = stacked([vert, down_map, courant[None]])
    columns = stacked([owner, counts])
    base, slot, steps, const = pl.pallas_call(
        functools.partial(local_kernel, cap, crm_z),
        in_specs=[VMEM] * 3,
        out_specs=[VMEM] * 4,
        out_shape=[f32(rows, col_dev), i32(1, col_dev), f32(SUBL, col_dev), f32(SUBL * crm_z, LANES)],
        compiler_params=params(),
        cost_estimate=pl.CostEstimate(flops=10**9, bytes_accessed=4 * 10**6, transcendentals=0),
        name="local",
    )(flat, maps, columns)

    dyn, outgoing = pl.pallas_call(
        functools.partial(send_kernel, crm_z),
        in_specs=[VMEM] * 8,
        out_specs=[VMEM] * 2,
        out_shape=[f32(rows, col_dev), f32(slots, LANES)],
        compiler_params=params(),
        name="send",
    )(base, slot, steps, maps, above, below, left, right)

    arrived = exchange(outgoing, devices)
    change = crm(const, arrived, crm_field, crm_z, crm_x)
    returned = exchange(change, devices)

    out = pl.pallas_call(
        final_kernel,
        in_specs=[VMEM] * 4,
        out_specs=VMEM,
        out_shape=f32(rows * width_x, width_y),
        compiler_params=params(),
        name="final",
    )(dyn, returned, slot, up_map)
    return out.reshape(state.shape)


def solution(mesh):
    in_specs = (
        P(None, "gx", "gy"),
        P("gx", "gy"),
        P("gx", "gy"),
        P(),
        P(),
        P(),
        P(),
        P(None, ("gx", "gy")),
    )
    out_specs = P(None, "gx", "gy")
    return jax.shard_map(body, mesh=mesh, in_specs=in_specs, out_specs=out_specs, check_vma=False)
```

```python
import functools
import math

import jax
import jax.numpy as jnp
from jax import lax
from jax.experimental import pallas as pl
from jax.experimental.pallas import tpu as pltpu
from jax.sharding import PartitionSpec as P

S_MAX = 4
DIFFUSION = 0.1
CONDENSE = 0.5
SLOPE = 0.3
LANES = 128
SUBL = 8
BETA = SLOPE * math.log2(math.e)
SHIFT = math.log2(BETA)

NT = (((1,), (1,)), ((), ()))
NN = (((1,), (0,)), ((), ()))
TN = (((0,), (0,)), ((), ()))


def split(value):
    high = value.astype(jnp.bfloat16)
    low = (value - high.astype(jnp.float32)).astype(jnp.bfloat16)
    return high, low


def dot(a, b, dims=NN):
    return lax.dot_general(a, b, dims, preferred_element_type=jnp.float32)


def dot3(a, b):
    a_hi, a_lo = split(a)
    b_hi, b_lo = split(b)
    return dot(a_hi, b_hi) + (dot(a_hi, b_lo) + dot(a_lo, b_hi))


def edges_kernel(state_ref, top_ref, bottom_ref, west_ref, east_ref):
    levels = top_ref.shape[0]
    rows = [state_ref[pl.ds(i, levels, stride=SUBL), :] for i in range(SUBL)]
    top_ref[...] = rows[0]
    bottom_ref[...] = rows[-1]
    row = lax.broadcasted_iota(jnp.int32, (SUBL, LANES), 0)
    lane = lax.broadcasted_iota(jnp.int32, (SUBL, LANES), 1)
    pick = ((row == 0) & (lane == 0)) | ((row == 1) & (lane == LANES - 1))
    pick = pick.astype(jnp.bfloat16)
    for i in range(SUBL):
        hi, lo = split(rows[i])
        side = dot(pick, hi, NT) + dot(pick, lo, NT)
        west_ref[i:i + 1, :] = side[0:1]
        east_ref[i:i + 1, :] = side[1:2]


def local_kernel(cap, crm_z, state_ref, small_ref, base_ref, slot_ref, steps_ref, const_ref):
    levels = base_ref.shape[0]
    half = levels // 2
    vert = small_ref[2 * SUBL:2 * SUBL + half, :half]
    wide = lax.broadcasted_iota(jnp.int32, (levels, LANES), 1)
    rows = [state_ref[pl.ds(i, levels, stride=SUBL), :] for i in range(SUBL)]
    laps = []
    for i in range(SUBL):
        mid = rows[i]
        lap = jnp.where(wide == 0, 0.0, pltpu.roll(mid, 1, 1))
        lap = lap + jnp.where(wide == LANES - 1, 0.0, pltpu.roll(mid, LANES - 1, 1))
        if i > 0:
            lap = lap + rows[i - 1]
        if i < SUBL - 1:
            lap = lap + rows[i + 1]
        laps.append(mid + DIFFUSION * (lap - 4.0 * mid))
    whole = jnp.concatenate(rows, axis=1)
    base = jnp.concatenate(laps, axis=1)
    base_ref[:half, :] = base[:half] + dot3(vert, whole[:half])
    base_ref[half:, :] = base[half:] + dot3(vert, whole[half:])

    owner = jnp.concatenate([small_ref[i:i + 1, :] for i in range(SUBL)], axis=1).astype(jnp.int32)
    width = owner.shape[1]
    devices = LANES * (-(-DEVICES // LANES))
    mine = lax.broadcasted_iota(jnp.int32, (devices, width), 0) == owner
    earlier = (
        lax.broadcasted_iota(jnp.int32, (width, width), 0)
        < lax.broadcasted_iota(jnp.int32, (width, width), 1)
    ).astype(jnp.bfloat16)
    before = dot(mine.astype(jnp.bfloat16), earlier)
    rank = jnp.sum(jnp.where(mine, before, 0.0), axis=0, keepdims=True).astype(jnp.int32)
    slot_ref[...] = owner * cap + rank
    counts = jnp.concatenate([small_ref[i:i + 1, :] for i in range(SUBL, 2 * SUBL)], axis=1)
    lead = (lax.broadcasted_iota(jnp.int32, (SUBL, width), 0) == 0).astype(jnp.float32)
    steps_ref[...] = lead * counts
    last = small_ref.shape[0] - SUBL
    line = jnp.broadcast_to(small_ref[last:last + 1, :], (LANES, LANES))
    c = line.T[:crm_z]
    keep = 1.0 - c
    for i, value in enumerate((BETA * keep, BETA * c, keep, c, 0.5 * keep, 0.5 * c)):
        const_ref[pl.ds(i, crm_z, stride=SUBL), :] = value


def send_kernel(
    crm_z, base_ref, slot_ref, steps_ref, small_ref, above_ref, below_ref, left_ref, right_ref,
    dyn_ref, out_ref,
):
    levels, width = base_ref.shape
    half = levels // 2
    pad_z = -(-crm_z // SUBL) * SUBL
    start = small_ref.shape[0] - SUBL - pad_z
    down = small_ref[start:start + pad_z, :half]
    sides = jnp.concatenate([left_ref[...], right_ref[...]], axis=0)
    row = lax.broadcasted_iota(jnp.int32, (2 * SUBL, width), 0)
    lane = lax.broadcasted_iota(jnp.int32, (2 * SUBL, width), 1)
    target = jnp.where(row < SUBL, row * LANES, (row - SUBL) * LANES + (LANES - 1))
    place = (lane == target).astype(jnp.bfloat16)
    s_hi, s_lo = split(sides)
    halo = dot(s_hi, place, TN) + dot(s_lo, place, TN)
    first = halo[:, :LANES] + above_ref[...]
    last = halo[:, width - LANES:] + below_ref[...]
    halo = jnp.concatenate([first, halo[:, LANES:width - LANES], last], axis=1)
    dyn = base_ref[...] + DIFFUSION * halo
    dyn_ref[...] = dyn
    prof_t = dot3(down, dyn[:half])
    prof_q = dot3(down, dyn[half:])
    blank = jnp.zeros((LANES - 2 * pad_z - SUBL, width), jnp.float32)
    payload = jnp.concatenate([prof_t, prof_q, steps_ref[...], blank], axis=0)
    p_hi, p_lo = split(payload)
    both = jnp.concatenate([p_hi, p_lo], axis=0)
    slot = slot_ref[...]
    chunk = out_ref.shape[0] // 2
    for start in range(0, out_ref.shape[0], chunk):
        ids = start + lax.broadcasted_iota(jnp.int32, (chunk, width), 0)
        sent = dot((ids == slot).astype(jnp.bfloat16), both, NT)
        out_ref[start:start + chunk, :] = sent[:, :LANES] + sent[:, LANES:]


def total(values):
    while len(values) > 1:
        values = [a + b for a, b in zip(values[::2], values[1::2])]
    return values[0]


def advect(values, stay, come):
    moved = [come * v for v in values]
    last = pltpu.roll(moved[-1], 1, 0)
    return [stay * v + m for v, m in zip(values, [last] + moved[:-1])]


def spread(ref, row):
    return jnp.broadcast_to(ref[pl.ds(row, 1), :], (SUBL, LANES))


def crm_kernel(
    crm_z, crm_x, blocks, const_ref, arrived_ref, field_hbm, out_ref,
    prof_ref, weight_ref, part_ref, turn_ref, buffers, sems,
):
    pad_z = -(-crm_z // SUBL) * SUBL
    quads = crm_x // SUBL
    half = LANES // 2
    block = pl.program_id(0)
    scale = 2.0 * CONDENSE / (BETA * crm_x)

    def rows_of(index, size):
        return pl.ds(pl.multiple_of(index * size, SUBL), size)

    def fetch(i):
        lanes = pl.ds(pl.multiple_of(i * LANES, LANES), LANES)
        side = lax.rem(i, 2)
        return pltpu.make_async_copy(field_hbm.at[:, lanes], buffers.at[side], sems.at[side])

    @pl.when(block == 0)
    def _():
        fetch(block).start()

        def unpack(i, carry):
            cols = arrived_ref[rows_of(i, LANES), :].T
            prof_ref[rows_of(2 * i, pad_z), :] = BETA * cols[:pad_z] + SHIFT
            prof_ref[rows_of(2 * i + 1, pad_z), :] = BETA * cols[pad_z:2 * pad_z]
            counts = cols[2 * pad_z:2 * pad_z + 1]
            part = jnp.where(counts > 3.0, 0.0625, jnp.where(counts > 2.0, 0.125, jnp.where(counts > 1.0, 0.25, 0.5)))
            weights = [(1.0 - part) * scale]
            weights += [jnp.where(counts > float(k), part * (-scale * 2.0**k), 0.0) for k in range(S_MAX)]
            weights += [jnp.zeros((SUBL - len(weights), LANES), jnp.float32)]
            weight_ref[rows_of(i, SUBL), :] = jnp.concatenate(weights, axis=0)
            return carry

        lax.fori_loop(0, blocks, unpack, 0, unroll=True)

    @pl.when(block + 1 < blocks)
    def _():
        fetch(block + 1).start()

    fetch(block).wait()
    field_ref = buffers.at[lax.rem(block, 2)]
    w_first, *w_kept = [spread(weight_ref, SUBL * block + i) for i in range(S_MAX + 1)]
    for z in range(crm_z):
        beta_keep, beta_c, keep, c, half_keep, half_c = [spread(const_ref, SUBL * z + i) for i in range(6)]
        base_t = spread(prof_ref, 2 * pad_z * block + z)
        base_q = spread(prof_ref, 2 * pad_z * block + pad_z + z)
        temper = [field_ref[pl.ds(z * crm_x + i, SUBL, stride=quads), :] for i in range(quads)]
        vapour = [field_ref[pl.ds((crm_z + z) * crm_x + i, SUBL, stride=quads), :] for i in range(quads)]
        temper = [t + base_t for t in advect(temper, beta_keep, beta_c)]
        vapour = [v + base_q for v in advect(vapour, beta_keep, beta_c)]
        sums = [t + v for t, v in zip(temper, vapour)]
        gone = w_first * total(vapour)
        for k in range(S_MAX):
            if k > 0:
                sums = advect(sums, keep, c)
                vapour = advect(vapour, half_keep, half_c)
                temper = [s - v for s, v in zip(sums, vapour)]
            kept = [jnp.minimum(v, jnp.exp2(t)) for t, v in zip(temper, vapour)]
            gone = gone + w_kept[k] * total(kept)
            if k < S_MAX - 1:
                vapour = [v + e for v, e in zip(vapour, kept)]
        part_ref[pl.ds(pl.multiple_of(SUBL * (pad_z * block + z), SUBL), SUBL), :] = gone

    @pl.when(block == blocks - 1)
    def _():
        lane = lax.broadcasted_iota(jnp.int32, (half, LANES), 1)
        level = lax.broadcasted_iota(jnp.int32, (half, LANES), 0)

        def pack(i, carry):
            start = i * (SUBL * pad_z)
            change = part_ref[pl.ds(start, pad_z, stride=SUBL), :]
            for j in range(1, SUBL):
                change = change + part_ref[pl.ds(start + j, pad_z, stride=SUBL), :]
            change = jnp.concatenate([change, jnp.zeros((half - pad_z, LANES), jnp.float32)], axis=0)
            change = jnp.where(level < crm_z, change, 0.0)
            turn_ref[rows_of(i, LANES), :] = jnp.concatenate([change, change], axis=0).T
            even = turn_ref[pl.ds(i * LANES, half, stride=2), :]
            odd = turn_ref[pl.ds(i * LANES + 1, half, stride=2), :]
            out_ref[rows_of(i, half), :] = jnp.where(lane < half, even, odd)
            return carry

        lax.fori_loop(0, blocks, pack, 0, unroll=True)


def final_kernel(dyn_ref, returned_ref, slot_ref, up_ref, out_hbm, out_ref, sems):
    half, crm_z = up_ref.shape
    slot = slot_ref[...]
    width = slot.shape[1]
    pairs = returned_ref.shape[0]
    r_hi, r_lo = split(returned_ref[...])
    both = jnp.concatenate([r_hi, r_lo], axis=1)
    ids = lax.broadcasted_iota(jnp.int32, (pairs, width), 0)
    pick = (ids == slot // 2).astype(jnp.bfloat16)
    got = dot(both, pick, TN)
    got = got[:LANES] + got[LANES:]
    change = jnp.where(slot % 2 == 0, got[:LANES // 2], got[LANES // 2:])
    up = jnp.concatenate([up_ref[...], jnp.zeros((half, LANES // 2 - crm_z), jnp.float32)], axis=1)
    tend = dot3(up, change)
    copies = []
    for v, new in enumerate((dyn_ref[:half, :] + tend, dyn_ref[half:, :] - tend)):
        for i in range(SUBL):
            out_ref[pl.ds(v * SUBL * half + i, half, stride=SUBL), :] = new[:, i * LANES:(i + 1) * LANES]
        rows = pl.ds(v * SUBL * half, SUBL * half)
        copies.append(pltpu.make_async_copy(out_ref.at[rows, :], out_hbm.at[rows, :], sems.at[v]))
        copies[-1].start()
    for copy in copies:
        copy.wait()


VMEM = pl.BlockSpec(memory_space=pltpu.VMEM)
DEVICES = 128


def params(limit_mib=16):
    return pltpu.CompilerParams(vmem_limit_bytes=limit_mib * 2**20)


def f32(*shape):
    return jax.ShapeDtypeStruct(shape, jnp.float32)


def i32(*shape):
    return jax.ShapeDtypeStruct(shape, jnp.int32)


def crm(const, arrived, crm_field, crm_z, crm_x):
    slots = arrived.shape[0]
    rows = crm_field.shape[0]
    blocks = slots // LANES
    pad_z = -(-crm_z // SUBL) * SUBL
    return pl.pallas_call(
        functools.partial(crm_kernel, crm_z, crm_x, blocks),
        grid=(blocks,),
        in_specs=[VMEM, VMEM, pl.BlockSpec(memory_space=pl.ANY)],
        out_specs=VMEM,
        out_shape=f32(slots // 2, LANES),
        scratch_shapes=[
            pltpu.VMEM((blocks * 2 * pad_z, LANES), jnp.float32),
            pltpu.VMEM((blocks * SUBL, LANES), jnp.float32),
            pltpu.VMEM((blocks * SUBL * pad_z, LANES), jnp.float32),
            pltpu.VMEM((slots, LANES), jnp.float32),
            pltpu.VMEM((2, rows, LANES), jnp.float32),
            pltpu.SemaphoreType.DMA((2,)),
        ],
        compiler_params=params(48),
        name="crm",
    )(const, arrived, crm_field)


def exchange(value, devices):
    sent = value.reshape(devices, 1, -1)
    got = lax.all_to_all(sent, ("gx", "gy"), split_axis=0, concat_axis=0, tiled=True)
    return got.reshape(value.shape)


def stacked(whole, real):
    values = [*whole, *real]
    tall = [-(-value.shape[0] // SUBL) * SUBL for value in values]
    parts, above = [], 0
    for value, height in zip(values, tall):
        below = sum(tall) - above - value.shape[0]
        parts.append(jnp.pad(value, ((above, below), (0, LANES - value.shape[1]))))
        above += height
    count = len(whole)
    return sum(parts[1:count], parts[0]).astype(jnp.float32) + sum(parts[count + 1:], parts[count])


def shifted(value, axis, step):
    count = lax.axis_size(axis)
    return lax.ppermute(value, axis, [(i, (i + step) % count) for i in range(count)])


def body(state, owner, counts, vert, down_map, up_map, courant, crm_field):
    rows, width_x, width_y = state.shape
    col_dev = width_x * width_y
    devices = lax.axis_size("gx") * lax.axis_size("gy")
    cap = max(2, 7 * col_dev // (4 * devices))
    slots = devices * cap
    crm_z = down_map.shape[0]
    crm_x = crm_field.shape[0] // (2 * crm_z)
    flat = state.reshape(rows * width_x, width_y)

    top, bottom, west, east = pl.pallas_call(
        edges_kernel,
        in_specs=[VMEM],
        out_specs=[VMEM] * 4,
        out_shape=[f32(rows, width_y), f32(rows, width_y), f32(width_x, rows), f32(width_x, rows)],
        compiler_params=params(),
        name="edges",
    )(flat)

    above = shifted(bottom, "gx", 1)
    below = shifted(top, "gx", -1)
    left = shifted(east, "gy", 1)
    right = shifted(west, "gy", -1)

    small = stacked([owner, counts], [vert, down_map, courant[None]])
    base, slot, steps, const = pl.pallas_call(
        functools.partial(local_kernel, cap, crm_z),
        in_specs=[VMEM] * 2,
        out_specs=[VMEM] * 4,
        out_shape=[f32(rows, col_dev), i32(1, col_dev), f32(SUBL, col_dev), f32(SUBL * crm_z, LANES)],
        compiler_params=params(),
        cost_estimate=pl.CostEstimate(flops=10**9, bytes_accessed=4 * 10**6, transcendentals=0),
        name="local",
    )(flat, small)

    dyn, outgoing = pl.pallas_call(
        functools.partial(send_kernel, crm_z),
        in_specs=[VMEM] * 8,
        out_specs=[VMEM] * 2,
        out_shape=[f32(rows, col_dev), f32(slots, LANES)],
        compiler_params=params(),
        name="send",
    )(base, slot, steps, small, above, below, left, right)

    arrived = exchange(outgoing, devices)
    change = crm(const, arrived, crm_field, crm_z, crm_x)
    returned = exchange(change, devices)

    out = pl.pallas_call(
        final_kernel,
        in_specs=[VMEM] * 4,
        out_specs=pl.BlockSpec(memory_space=pl.ANY),
        out_shape=f32(rows * width_x, width_y),
        scratch_shapes=[
            pltpu.VMEM((rows * width_x, width_y), jnp.float32),
            pltpu.SemaphoreType.DMA((2,)),
        ],
        compiler_params=params(),
        name="final",
    )(dyn, returned, slot, up_map)
    return out.reshape(state.shape)


def solution(mesh):
    in_specs = (
        P(None, "gx", "gy"),
        P("gx", "gy"),
        P("gx", "gy"),
        P(),
        P(),
        P(),
        P(),
        P(None, ("gx", "gy")),
    )
    out_specs = P(None, "gx", "gy")
    return jax.shard_map(body, mesh=mesh, in_specs=in_specs, out_specs=out_specs, check_vma=False)
```

```python
import functools
import math

import jax
import jax.numpy as jnp
from jax import lax
from jax.experimental import pallas as pl
from jax.experimental.pallas import tpu as pltpu
from jax.sharding import PartitionSpec as P

S_MAX = 4
DIFFUSION = 0.1
CONDENSE = 0.5
SLOPE = 0.3
LANES = 128
SUBL = 8
BETA = SLOPE * math.log2(math.e)
SHIFT = math.log2(BETA)

NT = (((1,), (1,)), ((), ()))
NN = (((1,), (0,)), ((), ()))
TN = (((0,), (0,)), ((), ()))


def split(value):
    high = value.astype(jnp.bfloat16)
    low = (value - high.astype(jnp.float32)).astype(jnp.bfloat16)
    return high, low


def dot(a, b, dims=NN):
    return lax.dot_general(a, b, dims, preferred_element_type=jnp.float32)


def dot3(a, b):
    a_hi, a_lo = split(a)
    b_hi, b_lo = split(b)
    return dot(a_hi, b_hi) + (dot(a_hi, b_lo) + dot(a_lo, b_hi))


def edges_kernel(state_ref, top_ref, bottom_ref, west_ref, east_ref):
    levels = top_ref.shape[0]
    rows = [state_ref[pl.ds(i, levels, stride=SUBL), :] for i in range(SUBL)]
    top_ref[...] = rows[0]
    bottom_ref[...] = rows[-1]
    row = lax.broadcasted_iota(jnp.int32, (SUBL, LANES), 0)
    lane = lax.broadcasted_iota(jnp.int32, (SUBL, LANES), 1)
    pick = ((row == 0) & (lane == 0)) | ((row == 1) & (lane == LANES - 1))
    pick = pick.astype(jnp.bfloat16)
    for i in range(SUBL):
        hi, lo = split(rows[i])
        side = dot(pick, hi, NT) + dot(pick, lo, NT)
        west_ref[i:i + 1, :] = side[0:1]
        east_ref[i:i + 1, :] = side[1:2]


def local_kernel(cap, crm_z, state_ref, small_ref, base_ref, slot_ref, sent_ref, edge_ref, const_ref):
    levels = base_ref.shape[0]
    half = levels // 2
    vert = small_ref[2 * SUBL:2 * SUBL + half, :half]
    wide = lax.broadcasted_iota(jnp.int32, (levels, LANES), 1)
    rows = [state_ref[pl.ds(i, levels, stride=SUBL), :] for i in range(SUBL)]
    laps = []
    for i in range(SUBL):
        mid = rows[i]
        lap = jnp.where(wide == 0, 0.0, pltpu.roll(mid, 1, 1))
        lap = lap + jnp.where(wide == LANES - 1, 0.0, pltpu.roll(mid, LANES - 1, 1))
        if i > 0:
            lap = lap + rows[i - 1]
        if i < SUBL - 1:
            lap = lap + rows[i + 1]
        laps.append(mid + DIFFUSION * (lap - 4.0 * mid))
    whole = jnp.concatenate(rows, axis=1)
    base = jnp.concatenate(laps, axis=1)
    temper = base[:half] + dot3(vert, whole[:half])
    vapour = base[half:] + dot3(vert, whole[half:])
    base_ref[:half, :] = temper
    base_ref[half:, :] = vapour

    owner = jnp.concatenate([small_ref[i:i + 1, :] for i in range(SUBL)], axis=1).astype(jnp.int32)
    width = owner.shape[1]
    devices = LANES * (-(-DEVICES // LANES))
    mine = lax.broadcasted_iota(jnp.int32, (devices, width), 0) == owner
    earlier = (
        lax.broadcasted_iota(jnp.int32, (width, width), 0)
        < lax.broadcasted_iota(jnp.int32, (width, width), 1)
    ).astype(jnp.bfloat16)
    before = dot(mine.astype(jnp.bfloat16), earlier)
    rank = jnp.sum(jnp.where(mine, before, 0.0), axis=0, keepdims=True).astype(jnp.int32)
    slot = owner * cap + rank
    slot_ref[...] = slot
    counts = jnp.concatenate([small_ref[i:i + 1, :] for i in range(SUBL, 2 * SUBL)], axis=1)
    lead = (lax.broadcasted_iota(jnp.int32, (SUBL, width), 0) == 0).astype(jnp.float32)
    both = payload(down_of(small_ref, crm_z, half), temper, vapour, lead * counts)
    chunk = sent_ref.shape[0] // 2
    for start in range(0, sent_ref.shape[0], chunk):
        ids = start + lax.broadcasted_iota(jnp.int32, (chunk, width), 0)
        sent = dot((ids == slot).astype(jnp.bfloat16), both, NT)
        sent_ref[start:start + chunk, :] = sent[:, :LANES] + sent[:, LANES:]
    digits = jnp.concatenate([(slot // LANES).astype(jnp.float32), (slot % LANES).astype(jnp.float32)], axis=0)
    ends = dot(digits.astype(jnp.bfloat16), ends_of(width), NT)
    ends = (ends[0:1] * LANES + ends[1:2]).astype(jnp.int32)
    ends = jnp.concatenate([ends, jnp.full((1, LANES - ends.shape[1]), -1, jnp.int32)], axis=1)
    edges = jnp.concatenate([slot[:, :LANES], slot[:, width - LANES:], ends], axis=1)
    ids = lax.broadcasted_iota(jnp.int32, edge_ref.shape, 0)
    edge_ref[...] = (ids == edges).astype(jnp.bfloat16)

    last = small_ref.shape[0] - SUBL
    line = jnp.broadcast_to(small_ref[last:last + 1, :], (LANES, LANES))
    c = line.T[:crm_z]
    keep = 1.0 - c
    for i, value in enumerate((BETA * keep, BETA * c, keep, c, 0.5 * keep, 0.5 * c)):
        const_ref[pl.ds(i, crm_z, stride=SUBL), :] = value


def ends_of(width):
    row = lax.broadcasted_iota(jnp.int32, (2 * SUBL, width), 0)
    lane = lax.broadcasted_iota(jnp.int32, (2 * SUBL, width), 1)
    target = jnp.where(row < SUBL, row * LANES, (row - SUBL) * LANES + (LANES - 1))
    return (lane == target).astype(jnp.bfloat16)


def down_of(small_ref, crm_z, half):
    pad_z = -(-crm_z // SUBL) * SUBL
    start = small_ref.shape[0] - SUBL - pad_z
    return small_ref[start:start + pad_z, :half]


def payload(down, temper, vapour, steps):
    parts = [dot3(down, temper), dot3(down, vapour), steps]
    blank = LANES - sum(part.shape[0] for part in parts)
    parts.append(jnp.zeros((blank, temper.shape[1]), jnp.float32))
    return jnp.concatenate(split(jnp.concatenate(parts, axis=0)), axis=0)


def send_kernel(crm_z, small_ref, sent_ref, edge_ref, above_ref, below_ref, left_ref, right_ref, out_ref):
    half = above_ref.shape[0] // 2
    sides = jnp.concatenate([left_ref[...], right_ref[...]], axis=0)
    row = lax.broadcasted_iota(jnp.int32, (2 * SUBL, LANES), 0)
    lane = lax.broadcasted_iota(jnp.int32, (2 * SUBL, LANES), 1)
    same = (row == lane).astype(jnp.bfloat16)
    s_hi, s_lo = split(sides)
    ends = dot(s_hi, same, TN) + dot(s_lo, same, TN)
    halo = DIFFUSION * jnp.concatenate([above_ref[...], below_ref[...], ends], axis=1)
    both = payload(down_of(small_ref, crm_z, half), halo[:half], halo[half:], jnp.zeros((SUBL, halo.shape[1]), jnp.float32))
    chunk = out_ref.shape[0] // 2
    for start in range(0, out_ref.shape[0], chunk):
        rows = slice(start, start + chunk)
        sent = dot(edge_ref[rows, :], both, NT)
        out_ref[rows, :] = sent_ref[rows, :] + (sent[:, :LANES] + sent[:, LANES:])


def halo_kernel(base_ref, above_ref, below_ref, left_ref, right_ref, dyn_ref):
    width = base_ref.shape[1]
    sides = jnp.concatenate([left_ref[...], right_ref[...]], axis=0)
    s_hi, s_lo = split(sides)
    place = ends_of(width)
    halo = dot(s_hi, place, TN) + dot(s_lo, place, TN)
    first = halo[:, :LANES] + above_ref[...]
    last = halo[:, width - LANES:] + below_ref[...]
    halo = jnp.concatenate([first, halo[:, LANES:width - LANES], last], axis=1)
    dyn_ref[...] = base_ref[...] + DIFFUSION * halo


def total(values):
    while len(values) > 1:
        values = [a + b for a, b in zip(values[::2], values[1::2])]
    return values[0]


def advect(values, stay, come):
    moved = [come * v for v in values]
    last = pltpu.roll(moved[-1], 1, 0)
    return [stay * v + m for v, m in zip(values, [last] + moved[:-1])]


def spread(ref, row):
    return jnp.broadcast_to(ref[pl.ds(row, 1), :], (SUBL, LANES))


def crm_kernel(
    crm_z, crm_x, blocks, const_ref, arrived_ref, field_hbm, out_ref,
    prof_ref, weight_ref, part_ref, pair_ref, turn_ref, buffers, sems,
):
    pad_z = -(-crm_z // SUBL) * SUBL
    quads = crm_x // SUBL
    half = LANES // 2
    block = pl.program_id(0)
    scale = 2.0 * CONDENSE / (BETA * crm_x)

    def rows_of(index, size):
        return pl.ds(pl.multiple_of(index * size, SUBL), size)

    def fetch(i):
        lanes = pl.ds(pl.multiple_of(i * LANES, LANES), LANES)
        side = lax.rem(i, 2)
        return pltpu.make_async_copy(field_hbm.at[:, lanes], buffers.at[side], sems.at[side])

    @pl.when(block == 0)
    def _():
        fetch(block).start()

        def unpack(i, carry):
            cols = arrived_ref[rows_of(i, LANES), :].T
            prof_ref[rows_of(2 * i, pad_z), :] = BETA * cols[:pad_z] + SHIFT
            prof_ref[rows_of(2 * i + 1, pad_z), :] = BETA * cols[pad_z:2 * pad_z]
            counts = cols[2 * pad_z:2 * pad_z + 1]
            part = jnp.where(counts > 3.0, 0.0625, jnp.where(counts > 2.0, 0.125, jnp.where(counts > 1.0, 0.25, 0.5)))
            weights = [(1.0 - part) * scale]
            weights += [jnp.where(counts > float(k), part * (-scale * 2.0**k), 0.0) for k in range(S_MAX)]
            weights += [jnp.zeros((SUBL - len(weights), LANES), jnp.float32)]
            weight_ref[rows_of(i, SUBL), :] = jnp.concatenate(weights, axis=0)
            return carry

        lax.fori_loop(0, blocks, unpack, 0, unroll=True)

    @pl.when(block + 1 < blocks)
    def _():
        fetch(block + 1).start()

    fetch(block).wait()
    field_ref = buffers.at[lax.rem(block, 2)]
    w_first, *w_kept = [spread(weight_ref, SUBL * block + i) for i in range(S_MAX + 1)]
    for z in range(crm_z):
        beta_keep, beta_c, keep, c, half_keep, half_c = [spread(const_ref, SUBL * z + i) for i in range(6)]
        base_t = spread(prof_ref, 2 * pad_z * block + z)
        base_q = spread(prof_ref, 2 * pad_z * block + pad_z + z)
        temper = [field_ref[pl.ds(z * crm_x + i, SUBL, stride=quads), :] for i in range(quads)]
        vapour = [field_ref[pl.ds((crm_z + z) * crm_x + i, SUBL, stride=quads), :] for i in range(quads)]
        temper = [t + base_t for t in advect(temper, beta_keep, beta_c)]
        vapour = [v + base_q for v in advect(vapour, beta_keep, beta_c)]
        sums = [t + v for t, v in zip(temper, vapour)]
        gone = w_first * total(vapour)
        for k in range(S_MAX):
            if k > 0:
                sums = advect(sums, keep, c)
                vapour = advect(vapour, half_keep, half_c)
                temper = [s - v for s, v in zip(sums, vapour)]
            kept = [jnp.minimum(v, jnp.exp2(t)) for t, v in zip(temper, vapour)]
            gone = gone + w_kept[k] * total(kept)
            if k < S_MAX - 1:
                vapour = [v + e for v, e in zip(vapour, kept)]
        part_ref[pl.ds(pl.multiple_of(SUBL * (pad_z * block + z), SUBL), SUBL), :] = gone

    @pl.when(block == blocks - 1)
    def _():
        lane = lax.broadcasted_iota(jnp.int32, (half, LANES), 1)
        level = lax.broadcasted_iota(jnp.int32, (half, LANES), 0)

        def pack(i, carry):
            start = i * (SUBL * pad_z)
            pairs = [part_ref[pl.ds(start + j, 2 * pad_z, stride=4), :] for j in range(4)]
            at = i * 2 * pad_z
            pair_ref[pl.ds(at, 2 * pad_z), :] = (pairs[0] + pairs[1]) + (pairs[2] + pairs[3])
            change = pair_ref[pl.ds(at, pad_z, stride=2), :] + pair_ref[pl.ds(at + 1, pad_z, stride=2), :]
            change = jnp.concatenate([change, jnp.zeros((half - pad_z, LANES), jnp.float32)], axis=0)
            change = jnp.where(level < crm_z, change, 0.0)
            turn_ref[rows_of(i, LANES), :] = jnp.concatenate([change, change], axis=0).T
            even = turn_ref[pl.ds(i * LANES, half, stride=2), :]
            odd = turn_ref[pl.ds(i * LANES + 1, half, stride=2), :]
            out_ref[rows_of(i, half), :] = jnp.where(lane < half, even, odd)
            return carry

        lax.fori_loop(0, blocks, pack, 0, unroll=True)


def final_kernel(dyn_ref, returned_ref, slot_ref, up_ref, out_hbm, out_ref, sems):
    half, crm_z = up_ref.shape
    slot = slot_ref[...]
    width = slot.shape[1]
    pairs = returned_ref.shape[0]
    r_hi, r_lo = split(returned_ref[...])
    both = jnp.concatenate([r_hi, r_lo], axis=1)
    ids = lax.broadcasted_iota(jnp.int32, (pairs, width), 0)
    pick = (ids == slot // 2).astype(jnp.bfloat16)
    got = dot(both, pick, TN)
    got = got[:LANES] + got[LANES:]
    change = jnp.where(slot % 2 == 0, got[:LANES // 2], got[LANES // 2:])
    up = jnp.concatenate([up_ref[...], jnp.zeros((half, LANES // 2 - crm_z), jnp.float32)], axis=1)
    tend = dot3(up, change)
    copies = []
    for v, new in enumerate((dyn_ref[:half, :] + tend, dyn_ref[half:, :] - tend)):
        for i in range(SUBL):
            out_ref[pl.ds(v * SUBL * half + i, half, stride=SUBL), :] = new[:, i * LANES:(i + 1) * LANES]
        rows = pl.ds(v * SUBL * half, SUBL * half)
        copies.append(pltpu.make_async_copy(out_ref.at[rows, :], out_hbm.at[rows, :], sems.at[v]))
        copies[-1].start()
    for copy in copies:
        copy.wait()


VMEM = pl.BlockSpec(memory_space=pltpu.VMEM)
DEVICES = 128


def params(limit_mib=16):
    return pltpu.CompilerParams(vmem_limit_bytes=limit_mib * 2**20)


def f32(*shape):
    return jax.ShapeDtypeStruct(shape, jnp.float32)


def i32(*shape):
    return jax.ShapeDtypeStruct(shape, jnp.int32)


def crm(const, arrived, crm_field, crm_z, crm_x):
    slots = arrived.shape[0]
    rows = crm_field.shape[0]
    blocks = slots // LANES
    pad_z = -(-crm_z // SUBL) * SUBL
    return pl.pallas_call(
        functools.partial(crm_kernel, crm_z, crm_x, blocks),
        grid=(blocks,),
        in_specs=[VMEM, VMEM, pl.BlockSpec(memory_space=pl.ANY)],
        out_specs=VMEM,
        out_shape=f32(slots // 2, LANES),
        scratch_shapes=[
            pltpu.VMEM((blocks * 2 * pad_z, LANES), jnp.float32),
            pltpu.VMEM((blocks * SUBL, LANES), jnp.float32),
            pltpu.VMEM((blocks * SUBL * pad_z, LANES), jnp.float32),
            pltpu.VMEM((blocks * 2 * pad_z, LANES), jnp.float32),
            pltpu.VMEM((slots, LANES), jnp.float32),
            pltpu.VMEM((2, rows, LANES), jnp.float32),
            pltpu.SemaphoreType.DMA((2,)),
        ],
        compiler_params=params(48),
        name="crm",
    )(const, arrived, crm_field)


def exchange(value, devices):
    sent = value.reshape(devices, 1, -1)
    got = lax.all_to_all(sent, ("gx", "gy"), split_axis=0, concat_axis=0, tiled=True)
    return got.reshape(value.shape)


def stacked(whole, real):
    values = [*whole, *real]
    tall = [-(-value.shape[0] // SUBL) * SUBL for value in values]
    parts, above = [], 0
    for value, height in zip(values, tall):
        below = sum(tall) - above - value.shape[0]
        parts.append(jnp.pad(value, ((above, below), (0, LANES - value.shape[1]))))
        above += height
    count = len(whole)
    return sum(parts[1:count], parts[0]).astype(jnp.float32) + sum(parts[count + 1:], parts[count])


def shifted(value, axis, step):
    count = lax.axis_size(axis)
    return lax.ppermute(value, axis, [(i, (i + step) % count) for i in range(count)])


def body(state, owner, counts, vert, down_map, up_map, courant, crm_field):
    rows, width_x, width_y = state.shape
    col_dev = width_x * width_y
    devices = lax.axis_size("gx") * lax.axis_size("gy")
    cap = max(2, 7 * col_dev // (4 * devices))
    slots = devices * cap
    crm_z = down_map.shape[0]
    crm_x = crm_field.shape[0] // (2 * crm_z)
    flat = state.reshape(rows * width_x, width_y)

    top, bottom, west, east = pl.pallas_call(
        edges_kernel,
        in_specs=[VMEM],
        out_specs=[VMEM] * 4,
        out_shape=[f32(rows, width_y), f32(rows, width_y), f32(width_x, rows), f32(width_x, rows)],
        compiler_params=params(),
        name="edges",
    )(flat)

    above = shifted(bottom, "gx", 1)
    below = shifted(top, "gx", -1)
    left = shifted(east, "gy", 1)
    right = shifted(west, "gy", -1)

    small = stacked([owner, counts], [vert, down_map, courant[None]])
    base, slot, sent, edge, const = pl.pallas_call(
        functools.partial(local_kernel, cap, crm_z),
        in_specs=[VMEM] * 2,
        out_specs=[VMEM] * 5,
        out_shape=[
            f32(rows, col_dev),
            i32(1, col_dev),
            f32(slots, LANES),
            jax.ShapeDtypeStruct((slots, 3 * LANES), jnp.bfloat16),
            f32(SUBL * crm_z, LANES),
        ],
        compiler_params=params(),
        cost_estimate=pl.CostEstimate(flops=10**9, bytes_accessed=4 * 10**6, transcendentals=0),
        name="local",
    )(flat, small)

    outgoing = pl.pallas_call(
        functools.partial(send_kernel, crm_z),
        in_specs=[VMEM] * 7,
        out_specs=VMEM,
        out_shape=f32(slots, LANES),
        compiler_params=params(),
        name="send",
    )(small, sent, edge, above, below, left, right)

    arrived = exchange(outgoing, devices)
    change = crm(const, arrived, crm_field, crm_z, crm_x)
    returned = exchange(change, devices)
    dyn = pl.pallas_call(
        halo_kernel,
        in_specs=[VMEM] * 5,
        out_specs=VMEM,
        out_shape=f32(rows, col_dev),
        compiler_params=params(),
        cost_estimate=pl.CostEstimate(flops=10**8, bytes_accessed=2 * 10**6, transcendentals=0),
        name="halo",
    )(base, above, below, left, right)

    out = pl.pallas_call(
        final_kernel,
        in_specs=[VMEM] * 4,
        out_specs=pl.BlockSpec(memory_space=pl.ANY),
        out_shape=f32(rows * width_x, width_y),
        scratch_shapes=[
            pltpu.VMEM((rows * width_x, width_y), jnp.float32),
            pltpu.SemaphoreType.DMA((2,)),
        ],
        compiler_params=params(),
        name="final",
    )(dyn, returned, slot, up_map)
    return out.reshape(state.shape)


def solution(mesh):
    in_specs = (
        P(None, "gx", "gy"),
        P("gx", "gy"),
        P("gx", "gy"),
        P(),
        P(),
        P(),
        P(),
        P(None, ("gx", "gy")),
    )
    out_specs = P(None, "gx", "gy")
    return jax.shard_map(body, mesh=mesh, in_specs=in_specs, out_specs=out_specs, check_vma=False)
```

```python
import functools
import math

import jax
import jax.numpy as jnp
from jax import lax
from jax.experimental import pallas as pl
from jax.experimental.pallas import tpu as pltpu
from jax.sharding import PartitionSpec as P

S_MAX = 4
DIFFUSION = 0.1
CONDENSE = 0.5
SLOPE = 0.3
LANES = 128
SUBL = 8
BETA = SLOPE * math.log2(math.e)
SHIFT = math.log2(BETA)

NT = (((1,), (1,)), ((), ()))
NN = (((1,), (0,)), ((), ()))
TN = (((0,), (0,)), ((), ()))


def split(value):
    high = value.astype(jnp.bfloat16)
    low = (value - high.astype(jnp.float32)).astype(jnp.bfloat16)
    return high, low


def dot(a, b, dims=NN):
    return lax.dot_general(a, b, dims, preferred_element_type=jnp.float32)


def dot3(a, b):
    depth = b.shape[0]
    pad = -depth % (2 * SUBL)
    if pad:
        a = jnp.concatenate([a, jnp.zeros((a.shape[0], pad), jnp.float32)], axis=1)
        b = jnp.concatenate([b, jnp.zeros((pad, b.shape[1]), jnp.float32)], axis=0)
    a_hi, a_lo = split(a)
    b_hi, b_lo = split(b)
    return dot(jnp.concatenate([a_hi, a_hi, a_lo], axis=1), jnp.concatenate([b_hi, b_lo, b_hi], axis=0))


def chosen(start, count, index):
    ids = start + lax.broadcasted_iota(jnp.int32, (count, index.shape[1]), 0)
    hit = ids.astype(jnp.int16) == index.astype(jnp.int16)
    return jnp.where(hit, jnp.bfloat16(1), jnp.bfloat16(0))


def edges_kernel(state_ref, top_ref, bottom_ref, west_ref, east_ref):
    levels = top_ref.shape[0]
    rows = [state_ref[pl.ds(i, levels, stride=SUBL), :] for i in range(SUBL)]
    top_ref[...] = rows[0]
    bottom_ref[...] = rows[-1]
    row = lax.broadcasted_iota(jnp.int32, (SUBL, LANES), 0)
    lane = lax.broadcasted_iota(jnp.int32, (SUBL, LANES), 1)
    pick = ((row == 0) & (lane == 0)) | ((row == 1) & (lane == LANES - 1))
    pick = pick.astype(jnp.bfloat16)
    for i in range(SUBL):
        hi, lo = split(rows[i])
        side = dot(pick, hi, NT) + dot(pick, lo, NT)
        west_ref[i:i + 1, :] = side[0:1]
        east_ref[i:i + 1, :] = side[1:2]


def local_kernel(cap, crm_z, state_ref, small_ref, base_ref, slot_ref, sent_ref, edge_ref, const_ref):
    levels = base_ref.shape[0]
    half = levels // 2
    vert = small_ref[2 * SUBL:2 * SUBL + half, :half]
    wide = lax.broadcasted_iota(jnp.int32, (levels, LANES), 1)
    rows = [state_ref[pl.ds(i, levels, stride=SUBL), :] for i in range(SUBL)]
    laps = []
    for i in range(SUBL):
        mid = rows[i]
        lap = jnp.where(wide == 0, 0.0, pltpu.roll(mid, 1, 1))
        lap = lap + jnp.where(wide == LANES - 1, 0.0, pltpu.roll(mid, LANES - 1, 1))
        if i > 0:
            lap = lap + rows[i - 1]
        if i < SUBL - 1:
            lap = lap + rows[i + 1]
        laps.append(mid + DIFFUSION * (lap - 4.0 * mid))
    whole = jnp.concatenate(rows, axis=1)
    base = jnp.concatenate(laps, axis=1)
    temper = base[:half] + dot3(vert, whole[:half])
    vapour = base[half:] + dot3(vert, whole[half:])
    base_ref[:half, :] = temper
    base_ref[half:, :] = vapour

    owner = jnp.concatenate([small_ref[i:i + 1, :] for i in range(SUBL)], axis=1).astype(jnp.int32)
    width = owner.shape[1]
    devices = LANES * (-(-DEVICES // LANES))
    mine = lax.broadcasted_iota(jnp.int32, (devices, width), 0) == owner
    line = lax.broadcasted_iota(jnp.int32, (LANES, 2 * LANES), 0)
    lane = lax.broadcasted_iota(jnp.int32, (LANES, 2 * LANES), 1)
    counting = ((line < lane) | (lane >= LANES)).astype(jnp.bfloat16)
    seen = jnp.zeros((devices, LANES), jnp.float32)
    ranks = []
    for i in range(SUBL):
        here = mine[:, i * LANES:(i + 1) * LANES]
        found = dot(here.astype(jnp.bfloat16), counting)
        ranks.append(jnp.sum(jnp.where(here, found[:, :LANES] + seen, 0.0), axis=0, keepdims=True))
        seen = seen + found[:, LANES:]
    rank = jnp.concatenate(ranks, axis=1).astype(jnp.int32)
    slot = owner * cap + rank
    slot_ref[...] = slot
    counts = jnp.concatenate([small_ref[i:i + 1, :] for i in range(SUBL, 2 * SUBL)], axis=1)
    lead = (lax.broadcasted_iota(jnp.int32, (SUBL, width), 0) == 0).astype(jnp.float32)
    both = payload(down_of(small_ref, crm_z, half), temper, vapour, lead * counts)
    chunk = sent_ref.shape[0] // 2
    for start in range(0, sent_ref.shape[0], chunk):
        sent = dot(chosen(start, chunk, slot), both, NT)
        sent_ref[start:start + chunk, :] = sent[:, :LANES] + sent[:, LANES:]
    digits = jnp.concatenate([(slot // LANES).astype(jnp.float32), (slot % LANES).astype(jnp.float32)], axis=0)
    ends = dot(digits.astype(jnp.bfloat16), ends_of(width), NT)
    ends = (ends[0:1] * LANES + ends[1:2]).astype(jnp.int32)
    ends = jnp.concatenate([ends, jnp.full((1, LANES - ends.shape[1]), -1, jnp.int32)], axis=1)
    edges = jnp.concatenate([slot[:, :LANES], slot[:, width - LANES:], ends], axis=1)
    edge_ref[...] = chosen(0, edge_ref.shape[0], edges)

    last = small_ref.shape[0] - SUBL
    line = jnp.broadcast_to(small_ref[last:last + 1, :], (LANES, LANES))
    c = line.T[:crm_z]
    keep = 1.0 - c
    for i, value in enumerate((BETA * keep, BETA * c, keep, c, 0.5 * keep, 0.5 * c)):
        const_ref[pl.ds(i, crm_z, stride=SUBL), :] = value


def ends_of(width):
    row = lax.broadcasted_iota(jnp.int32, (2 * SUBL, width), 0)
    lane = lax.broadcasted_iota(jnp.int32, (2 * SUBL, width), 1)
    target = jnp.where(row < SUBL, row * LANES, (row - SUBL) * LANES + (LANES - 1))
    return (lane == target).astype(jnp.bfloat16)


def down_of(small_ref, crm_z, half):
    pad_z = -(-crm_z // SUBL) * SUBL
    start = small_ref.shape[0] - SUBL - pad_z
    return small_ref[start:start + pad_z, :half]


def payload(down, temper, vapour, steps):
    parts = [dot3(down, temper), dot3(down, vapour), steps]
    blank = LANES - sum(part.shape[0] for part in parts)
    parts.append(jnp.zeros((blank, temper.shape[1]), jnp.float32))
    return jnp.concatenate(split(jnp.concatenate(parts, axis=0)), axis=0)


def send_kernel(crm_z, small_ref, sent_ref, edge_ref, above_ref, below_ref, left_ref, right_ref, out_ref):
    half = above_ref.shape[0] // 2
    sides = jnp.concatenate([left_ref[...], right_ref[...]], axis=0)
    row = lax.broadcasted_iota(jnp.int32, (2 * SUBL, LANES), 0)
    lane = lax.broadcasted_iota(jnp.int32, (2 * SUBL, LANES), 1)
    same = (row == lane).astype(jnp.bfloat16)
    s_hi, s_lo = split(sides)
    ends = dot(s_hi, same, TN) + dot(s_lo, same, TN)
    halo = DIFFUSION * jnp.concatenate([above_ref[...], below_ref[...], ends], axis=1)
    both = payload(down_of(small_ref, crm_z, half), halo[:half], halo[half:], jnp.zeros((SUBL, halo.shape[1]), jnp.float32))
    chunk = out_ref.shape[0] // 2
    for start in range(0, out_ref.shape[0], chunk):
        rows = slice(start, start + chunk)
        sent = dot(edge_ref[rows, :], both, NT)
        out_ref[rows, :] = sent_ref[rows, :] + (sent[:, :LANES] + sent[:, LANES:])


def halo_kernel(base_ref, above_ref, below_ref, left_ref, right_ref, dyn_ref):
    width = base_ref.shape[1]
    sides = jnp.concatenate([left_ref[...], right_ref[...]], axis=0)
    s_hi, s_lo = split(sides)
    place = ends_of(width)
    halo = dot(s_hi, place, TN) + dot(s_lo, place, TN)
    first = halo[:, :LANES] + above_ref[...]
    last = halo[:, width - LANES:] + below_ref[...]
    halo = jnp.concatenate([first, halo[:, LANES:width - LANES], last], axis=1)
    dyn_ref[...] = base_ref[...] + DIFFUSION * halo


def total(values):
    while len(values) > 1:
        values = [a + b for a, b in zip(values[::2], values[1::2])]
    return values[0]


def advect(values, stay, come):
    moved = [come * v for v in values]
    last = pltpu.roll(moved[-1], 1, 0)
    return [stay * v + m for v, m in zip(values, [last] + moved[:-1])]


def spread(ref, row):
    return jnp.broadcast_to(ref[pl.ds(row, 1), :], (SUBL, LANES))


def crm_kernel(
    crm_z, crm_x, blocks, const_ref, arrived_ref, field_hbm, out_ref,
    prof_ref, weight_ref, part_ref, pair_ref, turn_ref, buffers, sems,
):
    pad_z = -(-crm_z // SUBL) * SUBL
    quads = crm_x // SUBL
    half = LANES // 2
    block = pl.program_id(0)
    scale = 2.0 * CONDENSE / (BETA * crm_x)

    def rows_of(index, size):
        return pl.ds(pl.multiple_of(index * size, SUBL), size)

    def fetch(i):
        lanes = pl.ds(pl.multiple_of(i * LANES, LANES), LANES)
        side = lax.rem(i, 2)
        return pltpu.make_async_copy(field_hbm.at[:, lanes], buffers.at[side], sems.at[side])

    @pl.when(block == 0)
    def _():
        fetch(block).start()

        def unpack(i, carry):
            cols = arrived_ref[rows_of(i, LANES), :].T
            prof_ref[rows_of(2 * i, pad_z), :] = BETA * cols[:pad_z] + SHIFT
            prof_ref[rows_of(2 * i + 1, pad_z), :] = BETA * cols[pad_z:2 * pad_z]
            counts = cols[2 * pad_z:2 * pad_z + 1]
            part = jnp.where(counts > 3.0, 0.0625, jnp.where(counts > 2.0, 0.125, jnp.where(counts > 1.0, 0.25, 0.5)))
            weights = [(1.0 - part) * scale]
            weights += [jnp.where(counts > float(k), part * (-scale * 2.0**k), 0.0) for k in range(S_MAX)]
            weights += [jnp.zeros((SUBL - len(weights), LANES), jnp.float32)]
            weight_ref[rows_of(i, SUBL), :] = jnp.concatenate(weights, axis=0)
            return carry

        lax.fori_loop(0, blocks, unpack, 0, unroll=True)

    @pl.when(block + 1 < blocks)
    def _():
        fetch(block + 1).start()

    fetch(block).wait()
    field_ref = buffers.at[lax.rem(block, 2)]
    w_first, *w_kept = [spread(weight_ref, SUBL * block + i) for i in range(S_MAX + 1)]
    for z in range(crm_z):
        beta_keep, beta_c, keep, c, half_keep, half_c = [spread(const_ref, SUBL * z + i) for i in range(6)]
        base_t = spread(prof_ref, 2 * pad_z * block + z)
        base_q = spread(prof_ref, 2 * pad_z * block + pad_z + z)
        temper = [field_ref[pl.ds(z * crm_x + i, SUBL, stride=quads), :] for i in range(quads)]
        vapour = [field_ref[pl.ds((crm_z + z) * crm_x + i, SUBL, stride=quads), :] for i in range(quads)]
        temper = [t + base_t for t in advect(temper, beta_keep, beta_c)]
        vapour = [v + base_q for v in advect(vapour, beta_keep, beta_c)]
        sums = [t + v for t, v in zip(temper, vapour)]
        gone = w_first * total(vapour)
        for k in range(S_MAX):
            if k > 0:
                sums = advect(sums, keep, c)
                vapour = advect(vapour, half_keep, half_c)
                temper = [s - v for s, v in zip(sums, vapour)]
            kept = [jnp.minimum(v, jnp.exp2(t)) for t, v in zip(temper, vapour)]
            gone = gone + w_kept[k] * total(kept)
            if k < S_MAX - 1:
                vapour = [v + e for v, e in zip(vapour, kept)]
        part_ref[pl.ds(pl.multiple_of(SUBL * (pad_z * block + z), SUBL), SUBL), :] = gone

    @pl.when(block == blocks - 1)
    def _():
        lane = lax.broadcasted_iota(jnp.int32, (half, LANES), 1)
        level = lax.broadcasted_iota(jnp.int32, (half, LANES), 0)

        def pack(i, carry):
            start = i * (SUBL * pad_z)
            pairs = [part_ref[pl.ds(start + j, 2 * pad_z, stride=4), :] for j in range(4)]
            at = i * 2 * pad_z
            pair_ref[pl.ds(at, 2 * pad_z), :] = (pairs[0] + pairs[1]) + (pairs[2] + pairs[3])
            change = pair_ref[pl.ds(at, pad_z, stride=2), :] + pair_ref[pl.ds(at + 1, pad_z, stride=2), :]
            change = jnp.concatenate([change, jnp.zeros((half - pad_z, LANES), jnp.float32)], axis=0)
            change = jnp.where(level < crm_z, change, 0.0)
            turn_ref[rows_of(i, LANES), :] = jnp.concatenate([change, change], axis=0).T
            even = turn_ref[pl.ds(i * LANES, half, stride=2), :]
            odd = turn_ref[pl.ds(i * LANES + 1, half, stride=2), :]
            out_ref[rows_of(i, half), :] = jnp.where(lane < half, even, odd)
            return carry

        lax.fori_loop(0, blocks, pack, 0, unroll=True)


def final_kernel(dyn_ref, returned_ref, slot_ref, up_ref, out_hbm, out_ref, sems):
    half, crm_z = up_ref.shape
    slot = slot_ref[...]
    width = slot.shape[1]
    pairs = returned_ref.shape[0]
    r_hi, r_lo = split(returned_ref[...])
    both = jnp.concatenate([r_hi, r_lo], axis=1)
    got = dot(both, chosen(0, pairs, slot // 2), TN)
    even = jnp.broadcast_to(slot % 2 == 0, (LANES // 2, width))
    c_hi, c_lo = [
        jnp.where(even, part[:LANES // 2], part[LANES // 2:]).astype(jnp.bfloat16) for part in (got[:LANES], got[LANES:])
    ]
    up = jnp.concatenate([up_ref[...], jnp.zeros((half, LANES // 2 - crm_z), jnp.float32)], axis=1)
    u_hi, u_lo = split(up)
    tend = dot(jnp.concatenate([u_hi, u_hi, u_lo], axis=1), jnp.concatenate([c_hi, c_lo, c_hi], axis=0))
    copies = []
    for v, new in enumerate((dyn_ref[:half, :] + tend, dyn_ref[half:, :] - tend)):
        for i in range(SUBL):
            out_ref[pl.ds(v * SUBL * half + i, half, stride=SUBL), :] = new[:, i * LANES:(i + 1) * LANES]
        rows = pl.ds(v * SUBL * half, SUBL * half)
        copies.append(pltpu.make_async_copy(out_ref.at[rows, :], out_hbm.at[rows, :], sems.at[v]))
        copies[-1].start()
    for copy in copies:
        copy.wait()


VMEM = pl.BlockSpec(memory_space=pltpu.VMEM)
DEVICES = 128


def params(limit_mib=16):
    return pltpu.CompilerParams(vmem_limit_bytes=limit_mib * 2**20)


def f32(*shape):
    return jax.ShapeDtypeStruct(shape, jnp.float32)


def i32(*shape):
    return jax.ShapeDtypeStruct(shape, jnp.int32)


def crm(const, arrived, crm_field, crm_z, crm_x):
    slots = arrived.shape[0]
    rows = crm_field.shape[0]
    blocks = slots // LANES
    pad_z = -(-crm_z // SUBL) * SUBL
    return pl.pallas_call(
        functools.partial(crm_kernel, crm_z, crm_x, blocks),
        grid=(blocks,),
        in_specs=[VMEM, VMEM, pl.BlockSpec(memory_space=pl.ANY)],
        out_specs=VMEM,
        out_shape=f32(slots // 2, LANES),
        scratch_shapes=[
            pltpu.VMEM((blocks * 2 * pad_z, LANES), jnp.float32),
            pltpu.VMEM((blocks * SUBL, LANES), jnp.float32),
            pltpu.VMEM((blocks * SUBL * pad_z, LANES), jnp.float32),
            pltpu.VMEM((blocks * 2 * pad_z, LANES), jnp.float32),
            pltpu.VMEM((slots, LANES), jnp.float32),
            pltpu.VMEM((2, rows, LANES), jnp.float32),
            pltpu.SemaphoreType.DMA((2,)),
        ],
        compiler_params=params(48),
        name="crm",
    )(const, arrived, crm_field)


def exchange(value, devices):
    sent = value.reshape(devices, 1, -1)
    got = lax.all_to_all(sent, ("gx", "gy"), split_axis=0, concat_axis=0, tiled=True)
    return got.reshape(value.shape)


def stacked(whole, real):
    values = [*whole, *real]
    tall = [-(-value.shape[0] // SUBL) * SUBL for value in values]
    parts, above = [], 0
    for value, height in zip(values, tall):
        below = sum(tall) - above - value.shape[0]
        parts.append(jnp.pad(value, ((above, below), (0, LANES - value.shape[1]))))
        above += height
    count = len(whole)
    return sum(parts[1:count], parts[0]).astype(jnp.float32) + sum(parts[count + 1:], parts[count])


def shifted(value, axis, step):
    count = lax.axis_size(axis)
    return lax.ppermute(value, axis, [(i, (i + step) % count) for i in range(count)])


def body(state, owner, counts, vert, down_map, up_map, courant, crm_field):
    rows, width_x, width_y = state.shape
    col_dev = width_x * width_y
    devices = lax.axis_size("gx") * lax.axis_size("gy")
    cap = max(2, 7 * col_dev // (4 * devices))
    slots = devices * cap
    crm_z = down_map.shape[0]
    crm_x = crm_field.shape[0] // (2 * crm_z)
    flat = state.reshape(rows * width_x, width_y)

    top, bottom, west, east = pl.pallas_call(
        edges_kernel,
        in_specs=[VMEM],
        out_specs=[VMEM] * 4,
        out_shape=[f32(rows, width_y), f32(rows, width_y), f32(width_x, rows), f32(width_x, rows)],
        compiler_params=params(),
        name="edges",
    )(flat)

    above = shifted(bottom, "gx", 1)
    below = shifted(top, "gx", -1)
    left = shifted(east, "gy", 1)
    right = shifted(west, "gy", -1)

    small = stacked([owner, counts], [vert, down_map, courant[None]])
    base, slot, sent, edge, const = pl.pallas_call(
        functools.partial(local_kernel, cap, crm_z),
        in_specs=[VMEM] * 2,
        out_specs=[VMEM] * 5,
        out_shape=[
            f32(rows, col_dev),
            i32(1, col_dev),
            f32(slots, LANES),
            jax.ShapeDtypeStruct((slots, 3 * LANES), jnp.bfloat16),
            f32(SUBL * crm_z, LANES),
        ],
        compiler_params=params(),
        cost_estimate=pl.CostEstimate(flops=10**9, bytes_accessed=4 * 10**6, transcendentals=0),
        name="local",
    )(flat, small)

    outgoing = pl.pallas_call(
        functools.partial(send_kernel, crm_z),
        in_specs=[VMEM] * 7,
        out_specs=VMEM,
        out_shape=f32(slots, LANES),
        compiler_params=params(),
        name="send",
    )(small, sent, edge, above, below, left, right)

    arrived = exchange(outgoing, devices)
    change = crm(const, arrived, crm_field, crm_z, crm_x)
    returned = exchange(change, devices)
    dyn = pl.pallas_call(
        halo_kernel,
        in_specs=[VMEM] * 5,
        out_specs=VMEM,
        out_shape=f32(rows, col_dev),
        compiler_params=params(),
        cost_estimate=pl.CostEstimate(flops=10**8, bytes_accessed=2 * 10**6, transcendentals=0),
        name="halo",
    )(base, above, below, left, right)

    out = pl.pallas_call(
        final_kernel,
        in_specs=[VMEM] * 4,
        out_specs=pl.BlockSpec(memory_space=pl.ANY),
        out_shape=f32(rows * width_x, width_y),
        scratch_shapes=[
            pltpu.VMEM((rows * width_x, width_y), jnp.float32),
            pltpu.SemaphoreType.DMA((2,)),
        ],
        compiler_params=params(),
        name="final",
    )(dyn, returned, slot, up_map)
    return out.reshape(state.shape)


def solution(mesh):
    in_specs = (
        P(None, "gx", "gy"),
        P("gx", "gy"),
        P("gx", "gy"),
        P(),
        P(),
        P(),
        P(),
        P(None, ("gx", "gy")),
    )
    out_specs = P(None, "gx", "gy")
    return jax.shard_map(body, mesh=mesh, in_specs=in_specs, out_specs=out_specs, check_vma=False)
```

```python
import functools
import math

import jax
import jax.numpy as jnp
from jax import lax
from jax.experimental import pallas as pl
from jax.experimental.pallas import tpu as pltpu
from jax.sharding import PartitionSpec as P

S_MAX = 4
DIFFUSION = 0.1
CONDENSE = 0.5
SLOPE = 0.3
LANES = 128
SUBL = 8
BETA = SLOPE * math.log2(math.e)
SHIFT = math.log2(BETA)

NT = (((1,), (1,)), ((), ()))
NN = (((1,), (0,)), ((), ()))
TN = (((0,), (0,)), ((), ()))


def split(value):
    high = value.astype(jnp.bfloat16)
    low = (value - high.astype(jnp.float32)).astype(jnp.bfloat16)
    return high, low


def dot(a, b, dims=NN):
    return lax.dot_general(a, b, dims, preferred_element_type=jnp.float32)


def dot3(a, b):
    depth = b.shape[0]
    pad = -depth % (2 * SUBL)
    if pad:
        a = jnp.concatenate([a, jnp.zeros((a.shape[0], pad), jnp.float32)], axis=1)
        b = jnp.concatenate([b, jnp.zeros((pad, b.shape[1]), jnp.float32)], axis=0)
    a_hi, a_lo = split(a)
    b_hi, b_lo = split(b)
    return dot(jnp.concatenate([a_hi, a_hi, a_lo], axis=1), jnp.concatenate([b_hi, b_lo, b_hi], axis=0))


def chosen(start, count, index):
    ids = start + lax.broadcasted_iota(jnp.int32, (count, index.shape[1]), 0)
    hit = ids.astype(jnp.int16) == index.astype(jnp.int16)
    return jnp.where(hit, jnp.bfloat16(1), jnp.bfloat16(0))


def edges_kernel(state_ref, top_ref, bottom_ref, west_ref, east_ref):
    levels = top_ref.shape[0]
    rows = [state_ref[pl.ds(i, levels, stride=SUBL), :] for i in range(SUBL)]
    top_ref[...] = rows[0]
    bottom_ref[...] = rows[-1]
    row = lax.broadcasted_iota(jnp.int32, (SUBL, LANES), 0)
    lane = lax.broadcasted_iota(jnp.int32, (SUBL, LANES), 1)
    pick = ((row == 0) & (lane == 0)) | ((row == 1) & (lane == LANES - 1))
    pick = pick.astype(jnp.bfloat16)
    for i in range(SUBL):
        hi, lo = split(rows[i])
        side = dot(pick, hi, NT) + dot(pick, lo, NT)
        west_ref[i:i + 1, :] = side[0:1]
        east_ref[i:i + 1, :] = side[1:2]


def local_kernel(cap, crm_z, state_ref, small_ref, base_ref, slot_ref, sent_ref, edge_ref, const_ref):
    levels = base_ref.shape[0]
    half = levels // 2
    vert = small_ref[2 * SUBL:2 * SUBL + half, :half]
    wide = lax.broadcasted_iota(jnp.int32, (levels, LANES), 1)
    rows = [state_ref[pl.ds(i, levels, stride=SUBL), :] for i in range(SUBL)]
    laps = []
    for i in range(SUBL):
        mid = rows[i]
        lap = jnp.where(wide == 0, 0.0, pltpu.roll(mid, 1, 1))
        lap = lap + jnp.where(wide == LANES - 1, 0.0, pltpu.roll(mid, LANES - 1, 1))
        if i > 0:
            lap = lap + rows[i - 1]
        if i < SUBL - 1:
            lap = lap + rows[i + 1]
        laps.append(mid + DIFFUSION * (lap - 4.0 * mid))
    whole = jnp.concatenate(rows, axis=1)
    base = jnp.concatenate(laps, axis=1)
    temper = base[:half] + dot3(vert, whole[:half])
    vapour = base[half:] + dot3(vert, whole[half:])
    base_ref[:half, :] = temper
    base_ref[half:, :] = vapour

    owner = jnp.concatenate([small_ref[i:i + 1, :] for i in range(SUBL)], axis=1).astype(jnp.int32)
    width = owner.shape[1]
    devices = LANES * (-(-DEVICES // LANES))
    mine = lax.broadcasted_iota(jnp.int32, (devices, width), 0) == owner
    line = lax.broadcasted_iota(jnp.int32, (LANES, 2 * LANES), 0)
    lane = lax.broadcasted_iota(jnp.int32, (LANES, 2 * LANES), 1)
    counting = ((line < lane) | (lane >= LANES)).astype(jnp.bfloat16)
    seen = jnp.zeros((devices, LANES), jnp.float32)
    ranks = []
    for i in range(SUBL):
        here = mine[:, i * LANES:(i + 1) * LANES]
        found = dot(here.astype(jnp.bfloat16), counting)
        ranks.append(jnp.sum(jnp.where(here, found[:, :LANES] + seen, 0.0), axis=0, keepdims=True))
        seen = seen + found[:, LANES:]
    rank = jnp.concatenate(ranks, axis=1).astype(jnp.int32)
    slot = owner * cap + rank
    slot_ref[...] = slot
    counts = jnp.concatenate([small_ref[i:i + 1, :] for i in range(SUBL, 2 * SUBL)], axis=1)
    lead = (lax.broadcasted_iota(jnp.int32, (SUBL, width), 0) == 0).astype(jnp.float32)
    both = payload(down_of(small_ref, crm_z, half), temper, vapour, lead * counts)
    chunk = sent_ref.shape[0] // 2
    for start in range(0, sent_ref.shape[0], chunk):
        sent = dot(chosen(start, chunk, slot), both, NT)
        sent_ref[start:start + chunk, :] = sent[:, :LANES] + sent[:, LANES:]
    digits = jnp.concatenate([(slot // LANES).astype(jnp.float32), (slot % LANES).astype(jnp.float32)], axis=0)
    ends = dot(digits.astype(jnp.bfloat16), ends_of(width), NT)
    ends = (ends[0:1] * LANES + ends[1:2]).astype(jnp.int32)
    ends = jnp.concatenate([ends, jnp.full((1, LANES - ends.shape[1]), -1, jnp.int32)], axis=1)
    edges = jnp.concatenate([slot[:, :LANES], slot[:, width - LANES:], ends], axis=1)
    edge_ref[...] = chosen(0, edge_ref.shape[0], edges)

    last = small_ref.shape[0] - SUBL
    line = jnp.broadcast_to(small_ref[last:last + 1, :], (LANES, LANES))
    pad_z = const_ref.shape[0] // 6
    c = line.T[:pad_z]
    keep = 1.0 - c
    for i, value in enumerate((BETA * keep, BETA * c, keep, c, 0.5 * keep, 0.5 * c)):
        const_ref[i * pad_z:(i + 1) * pad_z, :] = value


def ends_of(width):
    row = lax.broadcasted_iota(jnp.int32, (2 * SUBL, width), 0)
    lane = lax.broadcasted_iota(jnp.int32, (2 * SUBL, width), 1)
    target = jnp.where(row < SUBL, row * LANES, (row - SUBL) * LANES + (LANES - 1))
    return (lane == target).astype(jnp.bfloat16)


def down_of(small_ref, crm_z, half):
    pad_z = -(-crm_z // SUBL) * SUBL
    start = small_ref.shape[0] - SUBL - pad_z
    return small_ref[start:start + pad_z, :half]


def payload(down, temper, vapour, steps):
    parts = [dot3(down, temper), dot3(down, vapour), steps]
    blank = LANES - sum(part.shape[0] for part in parts)
    parts.append(jnp.zeros((blank, temper.shape[1]), jnp.float32))
    return jnp.concatenate(split(jnp.concatenate(parts, axis=0)), axis=0)


def send_kernel(crm_z, small_ref, sent_ref, edge_ref, above_ref, below_ref, left_ref, right_ref, out_ref):
    half = above_ref.shape[0] // 2
    sides = jnp.concatenate([left_ref[...], right_ref[...]], axis=0)
    row = lax.broadcasted_iota(jnp.int32, (2 * SUBL, LANES), 0)
    lane = lax.broadcasted_iota(jnp.int32, (2 * SUBL, LANES), 1)
    same = (row == lane).astype(jnp.bfloat16)
    s_hi, s_lo = split(sides)
    ends = dot(s_hi, same, TN) + dot(s_lo, same, TN)
    halo = DIFFUSION * jnp.concatenate([above_ref[...], below_ref[...], ends], axis=1)
    both = payload(down_of(small_ref, crm_z, half), halo[:half], halo[half:], jnp.zeros((SUBL, halo.shape[1]), jnp.float32))
    chunk = out_ref.shape[0] // 2
    for start in range(0, out_ref.shape[0], chunk):
        rows = slice(start, start + chunk)
        sent = dot(edge_ref[rows, :], both, NT)
        out_ref[rows, :] = sent_ref[rows, :] + (sent[:, :LANES] + sent[:, LANES:])


def halo_kernel(base_ref, above_ref, below_ref, left_ref, right_ref, dyn_ref):
    width = base_ref.shape[1]
    sides = jnp.concatenate([left_ref[...], right_ref[...]], axis=0)
    s_hi, s_lo = split(sides)
    place = ends_of(width)
    halo = dot(s_hi, place, TN) + dot(s_lo, place, TN)
    first = halo[:, :LANES] + above_ref[...]
    last = halo[:, width - LANES:] + below_ref[...]
    halo = jnp.concatenate([first, halo[:, LANES:width - LANES], last], axis=1)
    dyn_ref[...] = base_ref[...] + DIFFUSION * halo


def substeps(count, load, wrap, coefs, base_t, base_q):
    beta_keep, beta_c, keep, c, half_keep, half_c = coefs
    raw = [load(p) for p in range(count)]
    temper, raw_q = [t for t, _ in raw], [q for _, q in raw]
    sums = [[None] * count for _ in range(S_MAX)]
    vapour = [[None] * count for _ in range(S_MAX)]
    first, kept_sums = None, [None] * S_MAX

    def mixed(values, p, stay, come):
        before = wrap(values[-1]) if p == 0 else values[p - 1]
        return stay * values[p] + come * before

    def plus(acc, value):
        return value if acc is None else acc + value

    for turn in range(count + S_MAX - 1):
        for k in range(S_MAX):
            if not k <= turn < count + k:
                continue
            p = turn % count
            if k == 0:
                t = mixed(temper, p, beta_keep, beta_c) + base_t
                q = mixed(raw_q, p, beta_keep, beta_c) + base_q
                s = t + q
                first = plus(first, q)
            else:
                s = mixed(sums[k - 1], p, keep, c)
                q = mixed(vapour[k - 1], p, half_keep, half_c)
                t = s - q
            kept = jnp.minimum(q, jnp.exp2(t))
            kept_sums[k] = plus(kept_sums[k], kept)
            if k < S_MAX - 1:
                sums[k][p] = s
                vapour[k][p] = q + kept
    return first, kept_sums


def crm_kernel(
    crm_z, crm_x, blocks, const_ref, arrived_ref, field_hbm, out_ref,
    prof_ref, weight_ref, part_ref, turn_ref, buffers, tails, sems,
):
    pad_z = -(-crm_z // SUBL) * SUBL
    groups, rest = crm_z // SUBL, crm_z % SUBL
    runs = SUBL // rest if rest else 1
    short = crm_x // runs
    half = LANES // 2
    block = pl.program_id(0)
    scale = 2.0 * CONDENSE / (BETA * crm_x)

    def rows_of(index, size):
        return pl.ds(pl.multiple_of(index * size, SUBL), size)

    starts = [sum(FETCHED[:i]) for i in range(len(FETCHED))]

    def refs_of(i):
        lanes = pl.ds(starts[i] * LANES, FETCHED[i] * LANES)
        own = pl.ds(starts[i], FETCHED[i])
        return buffers.at[:, :, :, lanes], tails.at[own]

    def fetch(i):
        lanes = pl.ds(starts[i] * LANES, FETCHED[i] * LANES)
        copies = []
        for v in range(2):
            full = field_hbm.at[v, pl.ds(0, groups * SUBL)].reshape(groups, SUBL, crm_x, field_hbm.shape[-1])
            for sub in range(SUBL):
                target = buffers.at[pl.ds(v * groups, groups), :, sub, lanes]
                copies.append(pltpu.make_async_copy(full.at[:, sub, :, lanes], target, sems.at[i]))
        for b in range(starts[i], starts[i] + FETCHED[i]):
            source = field_hbm.at[:, pl.ds(groups * SUBL, rest), :, pl.ds(b * LANES, LANES)]
            copies.append(pltpu.make_async_copy(source, tails.at[b], sems.at[i]))
        for copy in copies:
            copy.start()

    @pl.when(block == 0)
    def _():
        fetch(0)

        def unpack(i, carry):
            cols = arrived_ref[rows_of(i, LANES), :].T
            prof_ref[rows_of(2 * i, pad_z), :] = BETA * cols[:pad_z] + SHIFT
            prof_ref[rows_of(2 * i + 1, pad_z), :] = BETA * cols[pad_z:2 * pad_z]
            counts = cols[2 * pad_z:2 * pad_z + 1]
            part = jnp.where(counts > 3.0, 0.0625, jnp.where(counts > 2.0, 0.125, jnp.where(counts > 1.0, 0.25, 0.5)))
            weights = [(1.0 - part) * scale]
            weights += [jnp.where(counts > float(k), part * (-scale * 2.0**k), 0.0) for k in range(S_MAX)]
            weights += [jnp.zeros((SUBL - len(weights), LANES), jnp.float32)]
            weight_ref[rows_of(i, SUBL), :] = jnp.concatenate(weights, axis=0)
            return carry

        lax.fori_loop(0, blocks, unpack, 0, unroll=True)

    for i, start in enumerate(starts):
        @pl.when(block == start)
        def _(i=i):
            if i + 1 < len(FETCHED):
                fetch(i + 1)
            for ref in refs_of(i):
                pltpu.make_async_copy(ref, ref, sems.at[i]).wait()

    own_lanes = pl.ds(pl.multiple_of(block * LANES, LANES), LANES)

    def spread(ref, row):
        return jnp.broadcast_to(ref[pl.ds(row, 1), :], (SUBL, LANES))

    w_first, *w_kept = [spread(weight_ref, SUBL * block + i) for i in range(S_MAX + 1)]

    def change_of(first, kept_sums):
        gone = w_first * first
        for w, kept in zip(w_kept, kept_sums):
            gone = gone + w * kept
        return gone

    sub = lax.broadcasted_iota(jnp.int32, (SUBL, LANES), 0)
    for g in range(groups):
        coefs = [const_ref[i * pad_z + SUBL * g:i * pad_z + SUBL * (g + 1), :] for i in range(6)]
        base_t = prof_ref[rows_of(2 * block * (pad_z // SUBL) + g, SUBL), :]
        base_q = prof_ref[rows_of((2 * block + 1) * (pad_z // SUBL) + g, SUBL), :]
        result = substeps(
            crm_x,
            lambda p: (buffers[g, p, :, own_lanes], buffers[groups + g, p, :, own_lanes]),
            lambda v: v, coefs, base_t, base_q,
        )
        part_ref[rows_of(block * (pad_z // SUBL) + g, SUBL), :] = change_of(*result)
    if rest:
        def runs_of(ref, row):
            value = spread(ref, row)
            for z in range(1, rest):
                value = jnp.where(sub >= z * runs, spread(ref, row + z), value)
            return value

        def wrap(value):
            around = pltpu.roll(value, (1 - runs) % SUBL, 0)
            return jnp.where(sub % runs == 0, around, pltpu.roll(value, 1, 0))

        tail = tails.at[block].reshape(2, rest * crm_x, LANES)
        z = SUBL * groups
        coefs = [runs_of(const_ref, i * pad_z + z) for i in range(6)]
        base_t = runs_of(prof_ref, 2 * block * pad_z + z)
        base_q = runs_of(prof_ref, (2 * block + 1) * pad_z + z)
        result = substeps(short, lambda p: tuple(tail[v, pl.ds(p, SUBL, stride=short), :] for v in range(2)), wrap, coefs, base_t, base_q)
        gone = change_of(*result)
        lines = [jnp.sum(gone[i * runs:(i + 1) * runs], axis=0, keepdims=True) for i in range(rest)]
        lines.append(jnp.zeros((SUBL - rest, LANES), jnp.float32))
        part_ref[rows_of(block * (pad_z // SUBL) + groups, SUBL), :] = jnp.concatenate(lines, axis=0)

    @pl.when(block == blocks - 1)
    def _():
        lane = lax.broadcasted_iota(jnp.int32, (half, LANES), 1)

        def pack(i, carry):
            change = part_ref[rows_of(i, pad_z), :]
            change = jnp.concatenate([change, jnp.zeros((half - pad_z, LANES), jnp.float32)], axis=0)
            turn_ref[rows_of(i, LANES), :] = jnp.concatenate([change, change], axis=0).T
            even = turn_ref[pl.ds(i * LANES, half, stride=2), :]
            odd = turn_ref[pl.ds(i * LANES + 1, half, stride=2), :]
            out_ref[rows_of(i, half), :] = jnp.where(lane < half, even, odd)
            return carry

        lax.fori_loop(0, blocks, pack, 0, unroll=True)


def final_kernel(dyn_ref, returned_ref, slot_ref, up_ref, out_hbm, out_ref, sems):
    half, crm_z = up_ref.shape
    slot = slot_ref[...]
    width = slot.shape[1]
    pairs = returned_ref.shape[0]
    r_hi, r_lo = split(returned_ref[...])
    both = jnp.concatenate([r_hi, r_lo], axis=1)
    got = dot(both, chosen(0, pairs, slot // 2), TN)
    even = jnp.broadcast_to(slot % 2 == 0, (LANES // 2, width))
    c_hi, c_lo = [
        jnp.where(even, part[:LANES // 2], part[LANES // 2:]).astype(jnp.bfloat16) for part in (got[:LANES], got[LANES:])
    ]
    up = jnp.concatenate([up_ref[...], jnp.zeros((half, LANES // 2 - crm_z), jnp.float32)], axis=1)
    u_hi, u_lo = split(up)
    tend = dot(jnp.concatenate([u_hi, u_hi, u_lo], axis=1), jnp.concatenate([c_hi, c_lo, c_hi], axis=0))
    copies = []
    for v, new in enumerate((dyn_ref[:half, :] + tend, dyn_ref[half:, :] - tend)):
        for i in range(SUBL):
            out_ref[pl.ds(v * SUBL * half + i, half, stride=SUBL), :] = new[:, i * LANES:(i + 1) * LANES]
        rows = pl.ds(v * SUBL * half, SUBL * half)
        copies.append(pltpu.make_async_copy(out_ref.at[rows, :], out_hbm.at[rows, :], sems.at[v]))
        copies[-1].start()
    for copy in copies:
        copy.wait()


VMEM = pl.BlockSpec(memory_space=pltpu.VMEM)
DEVICES = 128
FETCHED = (1, 3, 5, 5)


def params(limit_mib=16):
    return pltpu.CompilerParams(vmem_limit_bytes=limit_mib * 2**20)


def f32(*shape):
    return jax.ShapeDtypeStruct(shape, jnp.float32)


def i32(*shape):
    return jax.ShapeDtypeStruct(shape, jnp.int32)


def crm(const, arrived, crm_field, crm_z, crm_x):
    slots = arrived.shape[0]
    blocks = slots // LANES
    pad_z = -(-crm_z // SUBL) * SUBL
    return pl.pallas_call(
        functools.partial(crm_kernel, crm_z, crm_x, blocks),
        grid=(blocks,),
        in_specs=[VMEM, VMEM, pl.BlockSpec(memory_space=pl.ANY)],
        out_specs=VMEM,
        out_shape=f32(slots // 2, LANES),
        scratch_shapes=[
            pltpu.VMEM((blocks * 2 * pad_z, LANES), jnp.float32),
            pltpu.VMEM((blocks * SUBL, LANES), jnp.float32),
            pltpu.VMEM((blocks * pad_z, LANES), jnp.float32),
            pltpu.VMEM((slots, LANES), jnp.float32),
            pltpu.VMEM((2 * (crm_z // SUBL), crm_x, SUBL, slots), jnp.float32),
            pltpu.VMEM((blocks, 2, crm_z % SUBL, crm_x, LANES), jnp.float32),
            pltpu.SemaphoreType.DMA((len(FETCHED),)),
        ],
        compiler_params=params(48),
        name="crm",
    )(const, arrived, crm_field.reshape(2, crm_z, crm_x, slots))


def exchange(value, devices):
    sent = value.reshape(devices, 1, -1)
    got = lax.all_to_all(sent, ("gx", "gy"), split_axis=0, concat_axis=0, tiled=True)
    return got.reshape(value.shape)


def stacked(whole, real):
    values = [*whole, *real]
    tall = [-(-value.shape[0] // SUBL) * SUBL for value in values]
    parts, above = [], 0
    for value, height in zip(values, tall):
        below = sum(tall) - above - value.shape[0]
        parts.append(jnp.pad(value, ((above, below), (0, LANES - value.shape[1]))))
        above += height
    count = len(whole)
    return sum(parts[1:count], parts[0]).astype(jnp.float32) + sum(parts[count + 1:], parts[count])


def shifted(value, axis, step):
    count = lax.axis_size(axis)
    return lax.ppermute(value, axis, [(i, (i + step) % count) for i in range(count)])


def body(state, owner, counts, vert, down_map, up_map, courant, crm_field):
    rows, width_x, width_y = state.shape
    col_dev = width_x * width_y
    devices = lax.axis_size("gx") * lax.axis_size("gy")
    cap = max(2, 7 * col_dev // (4 * devices))
    slots = devices * cap
    crm_z = down_map.shape[0]
    crm_x = crm_field.shape[0] // (2 * crm_z)
    flat = state.reshape(rows * width_x, width_y)

    top, bottom, west, east = pl.pallas_call(
        edges_kernel,
        in_specs=[VMEM],
        out_specs=[VMEM] * 4,
        out_shape=[f32(rows, width_y), f32(rows, width_y), f32(width_x, rows), f32(width_x, rows)],
        compiler_params=params(),
        name="edges",
    )(flat)

    above = shifted(bottom, "gx", 1)
    below = shifted(top, "gx", -1)
    left = shifted(east, "gy", 1)
    right = shifted(west, "gy", -1)

    small = stacked([owner, counts], [vert, down_map, courant[None]])
    base, slot, sent, edge, const = pl.pallas_call(
        functools.partial(local_kernel, cap, crm_z),
        in_specs=[VMEM] * 2,
        out_specs=[VMEM] * 5,
        out_shape=[
            f32(rows, col_dev),
            i32(1, col_dev),
            f32(slots, LANES),
            jax.ShapeDtypeStruct((slots, 3 * LANES), jnp.bfloat16),
            f32(6 * (-(-crm_z // SUBL) * SUBL), LANES),
        ],
        compiler_params=params(),
        cost_estimate=pl.CostEstimate(flops=10**9, bytes_accessed=4 * 10**6, transcendentals=0),
        name="local",
    )(flat, small)

    outgoing = pl.pallas_call(
        functools.partial(send_kernel, crm_z),
        in_specs=[VMEM] * 7,
        out_specs=VMEM,
        out_shape=f32(slots, LANES),
        compiler_params=params(),
        name="send",
    )(small, sent, edge, above, below, left, right)

    arrived = exchange(outgoing, devices)
    change = crm(const, arrived, crm_field, crm_z, crm_x)
    returned = exchange(change, devices)
    dyn = pl.pallas_call(
        halo_kernel,
        in_specs=[VMEM] * 5,
        out_specs=VMEM,
        out_shape=f32(rows, col_dev),
        compiler_params=params(),
        cost_estimate=pl.CostEstimate(flops=10**8, bytes_accessed=2 * 10**6, transcendentals=0),
        name="halo",
    )(base, above, below, left, right)

    out = pl.pallas_call(
        final_kernel,
        in_specs=[VMEM] * 4,
        out_specs=pl.BlockSpec(memory_space=pl.ANY),
        out_shape=f32(rows * width_x, width_y),
        scratch_shapes=[
            pltpu.VMEM((rows * width_x, width_y), jnp.float32),
            pltpu.SemaphoreType.DMA((2,)),
        ],
        compiler_params=params(),
        name="final",
    )(dyn, returned, slot, up_map)
    return out.reshape(state.shape)


def solution(mesh):
    in_specs = (
        P(None, "gx", "gy"),
        P("gx", "gy"),
        P("gx", "gy"),
        P(),
        P(),
        P(),
        P(),
        P(None, ("gx", "gy")),
    )
    out_specs = P(None, "gx", "gy")
    return jax.shard_map(body, mesh=mesh, in_specs=in_specs, out_specs=out_specs, check_vma=False)
```

```python
import functools
import math

import jax
import jax.numpy as jnp
from jax import lax
from jax.experimental import pallas as pl
from jax.experimental.pallas import tpu as pltpu
from jax.sharding import PartitionSpec as P

S_MAX = 4
DIFFUSION = 0.1
CONDENSE = 0.5
SLOPE = 0.3
LANES = 128
SUBL = 8
BETA = SLOPE * math.log2(math.e)
SHIFT = math.log2(BETA)

NT = (((1,), (1,)), ((), ()))
NN = (((1,), (0,)), ((), ()))
TN = (((0,), (0,)), ((), ()))


def split(value):
    high = value.astype(jnp.bfloat16)
    low = (value - high.astype(jnp.float32)).astype(jnp.bfloat16)
    return high, low


def dot(a, b, dims=NN):
    return lax.dot_general(a, b, dims, preferred_element_type=jnp.float32)


def dot3(a, b):
    depth = b.shape[0]
    pad = -depth % (2 * SUBL)
    if pad:
        a = jnp.concatenate([a, jnp.zeros((a.shape[0], pad), jnp.float32)], axis=1)
        b = jnp.concatenate([b, jnp.zeros((pad, b.shape[1]), jnp.float32)], axis=0)
    a_hi, a_lo = split(a)
    b_hi, b_lo = split(b)
    return dot(jnp.concatenate([a_hi, a_hi, a_lo], axis=1), jnp.concatenate([b_hi, b_lo, b_hi], axis=0))


def chosen(start, count, index):
    ids = start + lax.broadcasted_iota(jnp.int32, (count, index.shape[1]), 0)
    hit = ids.astype(jnp.int16) == index.astype(jnp.int16)
    return jnp.where(hit, jnp.bfloat16(1), jnp.bfloat16(0))


def edges_kernel(state_ref, top_ref, bottom_ref, west_ref, east_ref):
    levels = top_ref.shape[0]
    rows = [state_ref[pl.ds(i, levels, stride=SUBL), :] for i in range(SUBL)]
    top_ref[...] = rows[0]
    bottom_ref[...] = rows[-1]
    row = lax.broadcasted_iota(jnp.int32, (SUBL, LANES), 0)
    lane = lax.broadcasted_iota(jnp.int32, (SUBL, LANES), 1)
    pick = ((row == 0) & (lane == 0)) | ((row == 1) & (lane == LANES - 1))
    pick = pick.astype(jnp.bfloat16)
    for i in range(SUBL):
        hi, lo = split(rows[i])
        side = dot(pick, hi, NT) + dot(pick, lo, NT)
        west_ref[i:i + 1, :] = side[0:1]
        east_ref[i:i + 1, :] = side[1:2]


def local_kernel(cap, crm_z, state_ref, small_ref, base_ref, slot_ref, sent_ref, edge_ref, const_ref):
    levels = base_ref.shape[0]
    half = levels // 2
    vert = small_ref[2 * SUBL:2 * SUBL + half, :half]
    wide = lax.broadcasted_iota(jnp.int32, (levels, LANES), 1)
    rows = [state_ref[pl.ds(i, levels, stride=SUBL), :] for i in range(SUBL)]
    laps = []
    for i in range(SUBL):
        mid = rows[i]
        lap = jnp.where(wide == 0, 0.0, pltpu.roll(mid, 1, 1))
        lap = lap + jnp.where(wide == LANES - 1, 0.0, pltpu.roll(mid, LANES - 1, 1))
        if i > 0:
            lap = lap + rows[i - 1]
        if i < SUBL - 1:
            lap = lap + rows[i + 1]
        laps.append(mid + DIFFUSION * (lap - 4.0 * mid))
    whole = jnp.concatenate(rows, axis=1)
    base = jnp.concatenate(laps, axis=1)
    temper = base[:half] + dot3(vert, whole[:half])
    vapour = base[half:] + dot3(vert, whole[half:])
    base_ref[:half, :] = temper
    base_ref[half:, :] = vapour

    owner = jnp.concatenate([small_ref[i:i + 1, :] for i in range(SUBL)], axis=1).astype(jnp.int32)
    width = owner.shape[1]
    devices = LANES * (-(-DEVICES // LANES))
    mine = lax.broadcasted_iota(jnp.int32, (devices, width), 0) == owner
    line = lax.broadcasted_iota(jnp.int32, (LANES, 2 * LANES), 0)
    lane = lax.broadcasted_iota(jnp.int32, (LANES, 2 * LANES), 1)
    counting = ((line < lane) | (lane >= LANES)).astype(jnp.bfloat16)
    seen = jnp.zeros((devices, LANES), jnp.float32)
    ranks = []
    for i in range(SUBL):
        here = mine[:, i * LANES:(i + 1) * LANES]
        found = dot(here.astype(jnp.bfloat16), counting)
        ranks.append(jnp.sum(jnp.where(here, found[:, :LANES] + seen, 0.0), axis=0, keepdims=True))
        seen = seen + found[:, LANES:]
    rank = jnp.concatenate(ranks, axis=1).astype(jnp.int32)
    slot = owner * cap + rank
    slot_ref[...] = slot
    counts = jnp.concatenate([small_ref[i:i + 1, :] for i in range(SUBL, 2 * SUBL)], axis=1)
    lead = (lax.broadcasted_iota(jnp.int32, (SUBL, width), 0) == 0).astype(jnp.float32)
    both = payload(down_of(small_ref, crm_z, half), temper, vapour, lead * counts)
    chunk = sent_ref.shape[0] // 2
    for start in range(0, sent_ref.shape[0], chunk):
        sent = dot(chosen(start, chunk, slot), both, NT)
        sent_ref[start:start + chunk, :] = sent[:, :LANES] + sent[:, LANES:]
    digits = jnp.concatenate([(slot // LANES).astype(jnp.float32), (slot % LANES).astype(jnp.float32)], axis=0)
    ends = dot(digits.astype(jnp.bfloat16), ends_of(width), NT)
    ends = (ends[0:1] * LANES + ends[1:2]).astype(jnp.int32)
    ends = jnp.concatenate([ends, jnp.full((1, LANES - ends.shape[1]), -1, jnp.int32)], axis=1)
    edges = jnp.concatenate([slot[:, :LANES], slot[:, width - LANES:], ends], axis=1)
    edge_ref[...] = chosen(0, edge_ref.shape[0], edges)

    last = small_ref.shape[0] - SUBL
    line = jnp.broadcast_to(small_ref[last:last + 1, :], (LANES, LANES))
    pad_z = const_ref.shape[0] // 6
    c = line.T[:pad_z]
    keep = 1.0 - c
    for i, value in enumerate((BETA * keep, BETA * c, keep, c, 0.5 * keep, 0.5 * c)):
        const_ref[i * pad_z:(i + 1) * pad_z, :] = value


def ends_of(width):
    row = lax.broadcasted_iota(jnp.int32, (2 * SUBL, width), 0)
    lane = lax.broadcasted_iota(jnp.int32, (2 * SUBL, width), 1)
    target = jnp.where(row < SUBL, row * LANES, (row - SUBL) * LANES + (LANES - 1))
    return (lane == target).astype(jnp.bfloat16)


def down_of(small_ref, crm_z, half):
    pad_z = -(-crm_z // SUBL) * SUBL
    start = small_ref.shape[0] - SUBL - pad_z
    return small_ref[start:start + pad_z, :half]


def payload(down, temper, vapour, steps):
    parts = [dot3(down, temper), dot3(down, vapour), steps]
    blank = LANES - sum(part.shape[0] for part in parts)
    parts.append(jnp.zeros((blank, temper.shape[1]), jnp.float32))
    return jnp.concatenate(split(jnp.concatenate(parts, axis=0)), axis=0)


def send_kernel(crm_z, small_ref, sent_ref, edge_ref, above_ref, below_ref, left_ref, right_ref, out_ref):
    half = above_ref.shape[0] // 2
    sides = jnp.concatenate([left_ref[...], right_ref[...]], axis=0)
    row = lax.broadcasted_iota(jnp.int32, (2 * SUBL, LANES), 0)
    lane = lax.broadcasted_iota(jnp.int32, (2 * SUBL, LANES), 1)
    same = (row == lane).astype(jnp.bfloat16)
    s_hi, s_lo = split(sides)
    ends = dot(s_hi, same, TN) + dot(s_lo, same, TN)
    down = down_of(small_ref, crm_z, half)

    def packed(halo):
        halo = DIFFUSION * halo
        return payload(down, halo[:half], halo[half:], jnp.zeros((SUBL, halo.shape[1]), jnp.float32))

    lines = packed(jnp.concatenate([above_ref[...], below_ref[...]], axis=1))
    ends = packed(ends)
    split_at = 2 * LANES
    chunk = out_ref.shape[0] // 2
    for start in range(0, out_ref.shape[0], chunk):
        rows = slice(start, start + chunk)
        sent = dot(edge_ref[rows, :split_at], lines, NT) + dot(edge_ref[rows, split_at:], ends, NT)
        out_ref[rows, :] = sent_ref[rows, :] + (sent[:, :LANES] + sent[:, LANES:])


def halo_kernel(base_ref, above_ref, below_ref, left_ref, right_ref, dyn_ref):
    width = base_ref.shape[1]
    sides = jnp.concatenate([left_ref[...], right_ref[...]], axis=0)
    s_hi, s_lo = split(sides)
    place = ends_of(width)
    halo = dot(s_hi, place, TN) + dot(s_lo, place, TN)
    first = halo[:, :LANES] + above_ref[...]
    last = halo[:, width - LANES:] + below_ref[...]
    halo = jnp.concatenate([first, halo[:, LANES:width - LANES], last], axis=1)
    dyn_ref[...] = base_ref[...] + DIFFUSION * halo


def substeps(count, load, wrap, coefs, base_t, base_q):
    beta_keep, beta_c, keep, c, half_keep, half_c = coefs
    raw = [load(p) for p in range(count)]
    temper, raw_q = [t for t, _ in raw], [q for _, q in raw]
    sums = [[None] * count for _ in range(S_MAX)]
    vapour = [[None] * count for _ in range(S_MAX)]
    first, kept_sums = None, [None] * S_MAX

    def mixed(values, p, stay, come):
        before = wrap(values[-1]) if p == 0 else values[p - 1]
        return stay * values[p] + come * before

    def plus(acc, value):
        return value if acc is None else acc + value

    for turn in range(count + S_MAX - 1):
        for k in range(S_MAX):
            if not k <= turn < count + k:
                continue
            p = turn % count
            if k == 0:
                t = mixed(temper, p, beta_keep, beta_c) + base_t
                q = mixed(raw_q, p, beta_keep, beta_c) + base_q
                s = t + q
                first = plus(first, q)
            else:
                s = mixed(sums[k - 1], p, keep, c)
                q = mixed(vapour[k - 1], p, half_keep, half_c)
                t = s - q
            kept = jnp.minimum(q, jnp.exp2(t))
            kept_sums[k] = plus(kept_sums[k], kept)
            if k < S_MAX - 1:
                sums[k][p] = s
                vapour[k][p] = q + kept
    return first, kept_sums


def crm_kernel(
    crm_z, crm_x, blocks, const_ref, arrived_ref, field_hbm, out_ref,
    prof_ref, weight_ref, part_ref, turn_ref, buffers, tails, sems,
):
    pad_z = -(-crm_z // SUBL) * SUBL
    groups, rest = crm_z // SUBL, crm_z % SUBL
    runs = SUBL // rest if rest else 1
    short = crm_x // runs
    half = LANES // 2
    block = pl.program_id(0)
    scale = 2.0 * CONDENSE / (BETA * crm_x)

    def rows_of(index, size):
        return pl.ds(pl.multiple_of(index * size, SUBL), size)

    starts = [sum(FETCHED[:i]) for i in range(len(FETCHED))]

    def refs_of(i):
        lanes = pl.ds(starts[i] * LANES, FETCHED[i] * LANES)
        own = pl.ds(starts[i], FETCHED[i])
        return buffers.at[:, :, :, lanes], tails.at[own]

    def fetch(i):
        lanes = pl.ds(starts[i] * LANES, FETCHED[i] * LANES)
        copies = []
        for v in range(2):
            full = field_hbm.at[v, pl.ds(0, groups * SUBL)].reshape(groups, SUBL, crm_x, field_hbm.shape[-1])
            for sub in range(SUBL):
                target = buffers.at[pl.ds(v * groups, groups), :, sub, lanes]
                copies.append(pltpu.make_async_copy(full.at[:, sub, :, lanes], target, sems.at[i]))
        for b in range(starts[i], starts[i] + FETCHED[i]):
            source = field_hbm.at[:, pl.ds(groups * SUBL, rest), :, pl.ds(b * LANES, LANES)]
            copies.append(pltpu.make_async_copy(source, tails.at[b], sems.at[i]))
        for copy in copies:
            copy.start()

    @pl.when(block == 0)
    def _():
        fetch(0)

        def unpack(i, carry):
            cols = arrived_ref[rows_of(i, LANES), :].T
            prof_ref[rows_of(2 * i, pad_z), :] = BETA * cols[:pad_z] + SHIFT
            prof_ref[rows_of(2 * i + 1, pad_z), :] = BETA * cols[pad_z:2 * pad_z]
            counts = cols[2 * pad_z:2 * pad_z + 1]
            part = jnp.where(counts > 3.0, 0.0625, jnp.where(counts > 2.0, 0.125, jnp.where(counts > 1.0, 0.25, 0.5)))
            weights = [(1.0 - part) * scale]
            weights += [jnp.where(counts > float(k), part * (-scale * 2.0**k), 0.0) for k in range(S_MAX)]
            weights += [jnp.zeros((SUBL - len(weights), LANES), jnp.float32)]
            weight_ref[rows_of(i, SUBL), :] = jnp.concatenate(weights, axis=0)
            return carry

        lax.fori_loop(0, blocks, unpack, 0, unroll=True)

    for i, start in enumerate(starts):
        @pl.when(block == start)
        def _(i=i):
            if i + 1 < len(FETCHED):
                fetch(i + 1)
            for ref in refs_of(i):
                pltpu.make_async_copy(ref, ref, sems.at[i]).wait()

    own_lanes = pl.ds(pl.multiple_of(block * LANES, LANES), LANES)

    def spread(ref, row):
        return jnp.broadcast_to(ref[pl.ds(row, 1), :], (SUBL, LANES))

    w_first, *w_kept = [spread(weight_ref, SUBL * block + i) for i in range(S_MAX + 1)]

    def change_of(first, kept_sums):
        gone = w_first * first
        for w, kept in zip(w_kept, kept_sums):
            gone = gone + w * kept
        return gone

    sub = lax.broadcasted_iota(jnp.int32, (SUBL, LANES), 0)
    for g in range(groups):
        coefs = [const_ref[i * pad_z + SUBL * g:i * pad_z + SUBL * (g + 1), :] for i in range(6)]
        base_t = prof_ref[rows_of(2 * block * (pad_z // SUBL) + g, SUBL), :]
        base_q = prof_ref[rows_of((2 * block + 1) * (pad_z // SUBL) + g, SUBL), :]
        result = substeps(
            crm_x,
            lambda p: (buffers[g, p, :, own_lanes], buffers[groups + g, p, :, own_lanes]),
            lambda v: v, coefs, base_t, base_q,
        )
        part_ref[rows_of(block * (pad_z // SUBL) + g, SUBL), :] = change_of(*result)
    if rest:
        def runs_of(ref, row):
            value = spread(ref, row)
            for z in range(1, rest):
                value = jnp.where(sub >= z * runs, spread(ref, row + z), value)
            return value

        def wrap(value):
            around = pltpu.roll(value, (1 - runs) % SUBL, 0)
            return jnp.where(sub % runs == 0, around, pltpu.roll(value, 1, 0))

        tail = tails.at[block].reshape(2, rest * crm_x, LANES)
        z = SUBL * groups
        coefs = [runs_of(const_ref, i * pad_z + z) for i in range(6)]
        base_t = runs_of(prof_ref, 2 * block * pad_z + z)
        base_q = runs_of(prof_ref, (2 * block + 1) * pad_z + z)
        result = substeps(short, lambda p: tuple(tail[v, pl.ds(p, SUBL, stride=short), :] for v in range(2)), wrap, coefs, base_t, base_q)
        gone = change_of(*result)
        lines = [jnp.sum(gone[i * runs:(i + 1) * runs], axis=0, keepdims=True) for i in range(rest)]
        lines.append(jnp.zeros((SUBL - rest, LANES), jnp.float32))
        part_ref[rows_of(block * (pad_z // SUBL) + groups, SUBL), :] = jnp.concatenate(lines, axis=0)

    @pl.when(block == blocks - 1)
    def _():
        lane = lax.broadcasted_iota(jnp.int32, (half, LANES), 1)

        def pack(i, carry):
            change = part_ref[rows_of(i, pad_z), :]
            change = jnp.concatenate([change, jnp.zeros((half - pad_z, LANES), jnp.float32)], axis=0)
            turn_ref[rows_of(i, LANES), :] = jnp.concatenate([change, change], axis=0).T
            even = turn_ref[pl.ds(i * LANES, half, stride=2), :]
            odd = turn_ref[pl.ds(i * LANES + 1, half, stride=2), :]
            out_ref[rows_of(i, half), :] = jnp.where(lane < half, even, odd)
            return carry

        lax.fori_loop(0, blocks, pack, 0, unroll=True)


def final_kernel(dyn_ref, returned_ref, slot_ref, up_ref, out_hbm, out_ref, sems):
    half, crm_z = up_ref.shape
    slot = slot_ref[...]
    width = slot.shape[1]
    pairs = returned_ref.shape[0]
    r_hi, r_lo = split(returned_ref[...])
    both = jnp.concatenate([r_hi, r_lo], axis=1)
    got = dot(both, chosen(0, pairs, slot // 2), TN)
    even = jnp.broadcast_to(slot % 2 == 0, (LANES // 2, width))
    c_hi, c_lo = [
        jnp.where(even, part[:LANES // 2], part[LANES // 2:]).astype(jnp.bfloat16) for part in (got[:LANES], got[LANES:])
    ]
    up = jnp.concatenate([up_ref[...], jnp.zeros((half, LANES // 2 - crm_z), jnp.float32)], axis=1)
    u_hi, u_lo = split(up)
    tend = dot(jnp.concatenate([u_hi, u_hi, u_lo], axis=1), jnp.concatenate([c_hi, c_lo, c_hi], axis=0))
    copies = []
    for v, new in enumerate((dyn_ref[:half, :] + tend, dyn_ref[half:, :] - tend)):
        for i in range(SUBL):
            out_ref[pl.ds(v * SUBL * half + i, half, stride=SUBL), :] = new[:, i * LANES:(i + 1) * LANES]
        rows = pl.ds(v * SUBL * half, SUBL * half)
        copies.append(pltpu.make_async_copy(out_ref.at[rows, :], out_hbm.at[rows, :], sems.at[v]))
        copies[-1].start()
    for copy in copies:
        copy.wait()


VMEM = pl.BlockSpec(memory_space=pltpu.VMEM)
DEVICES = 128
FETCHED = (1, 3, 5, 5)


def params(limit_mib=16):
    return pltpu.CompilerParams(vmem_limit_bytes=limit_mib * 2**20)


def f32(*shape):
    return jax.ShapeDtypeStruct(shape, jnp.float32)


def i32(*shape):
    return jax.ShapeDtypeStruct(shape, jnp.int32)


def crm(const, arrived, crm_field, crm_z, crm_x):
    slots = arrived.shape[0]
    blocks = slots // LANES
    pad_z = -(-crm_z // SUBL) * SUBL
    return pl.pallas_call(
        functools.partial(crm_kernel, crm_z, crm_x, blocks),
        grid=(blocks,),
        in_specs=[VMEM, VMEM, pl.BlockSpec(memory_space=pl.ANY)],
        out_specs=VMEM,
        out_shape=f32(slots // 2, LANES),
        scratch_shapes=[
            pltpu.VMEM((blocks * 2 * pad_z, LANES), jnp.float32),
            pltpu.VMEM((blocks * SUBL, LANES), jnp.float32),
            pltpu.VMEM((blocks * pad_z, LANES), jnp.float32),
            pltpu.VMEM((slots, LANES), jnp.float32),
            pltpu.VMEM((2 * (crm_z // SUBL), crm_x, SUBL, slots), jnp.float32),
            pltpu.VMEM((blocks, 2, crm_z % SUBL, crm_x, LANES), jnp.float32),
            pltpu.SemaphoreType.DMA((len(FETCHED),)),
        ],
        compiler_params=params(48),
        name="crm",
    )(const, arrived, crm_field.reshape(2, crm_z, crm_x, slots))


def exchange(value, devices):
    sent = value.reshape(devices, 1, -1)
    got = lax.all_to_all(sent, ("gx", "gy"), split_axis=0, concat_axis=0, tiled=True)
    return got.reshape(value.shape)


def stacked(whole, real):
    values = [*whole, *real]
    tall = [-(-value.shape[0] // SUBL) * SUBL for value in values]
    parts, above = [], 0
    for value, height in zip(values, tall):
        below = sum(tall) - above - value.shape[0]
        parts.append(jnp.pad(value, ((above, below), (0, LANES - value.shape[1]))))
        above += height
    count = len(whole)
    return sum(parts[1:count], parts[0]).astype(jnp.float32) + sum(parts[count + 1:], parts[count])


def shifted(value, axis, step):
    count = lax.axis_size(axis)
    return lax.ppermute(value, axis, [(i, (i + step) % count) for i in range(count)])


def body(state, owner, counts, vert, down_map, up_map, courant, crm_field):
    rows, width_x, width_y = state.shape
    col_dev = width_x * width_y
    devices = lax.axis_size("gx") * lax.axis_size("gy")
    cap = max(2, 7 * col_dev // (4 * devices))
    slots = devices * cap
    crm_z = down_map.shape[0]
    crm_x = crm_field.shape[0] // (2 * crm_z)
    flat = state.reshape(rows * width_x, width_y)

    top, bottom, west, east = pl.pallas_call(
        edges_kernel,
        in_specs=[VMEM],
        out_specs=[VMEM] * 4,
        out_shape=[f32(rows, width_y), f32(rows, width_y), f32(width_x, rows), f32(width_x, rows)],
        compiler_params=params(),
        name="edges",
    )(flat)

    above = shifted(bottom, "gx", 1)
    below = shifted(top, "gx", -1)
    left = shifted(east, "gy", 1)
    right = shifted(west, "gy", -1)

    small = stacked([owner, counts], [vert, down_map, courant[None]])
    base, slot, sent, edge, const = pl.pallas_call(
        functools.partial(local_kernel, cap, crm_z),
        in_specs=[VMEM] * 2,
        out_specs=[VMEM] * 5,
        out_shape=[
            f32(rows, col_dev),
            i32(1, col_dev),
            f32(slots, LANES),
            jax.ShapeDtypeStruct((slots, 3 * LANES), jnp.bfloat16),
            f32(6 * (-(-crm_z // SUBL) * SUBL), LANES),
        ],
        compiler_params=params(),
        cost_estimate=pl.CostEstimate(flops=10**9, bytes_accessed=4 * 10**6, transcendentals=0),
        name="local",
    )(flat, small)

    outgoing = pl.pallas_call(
        functools.partial(send_kernel, crm_z),
        in_specs=[VMEM] * 7,
        out_specs=VMEM,
        out_shape=f32(slots, LANES),
        compiler_params=params(),
        name="send",
    )(small, sent, edge, above, below, left, right)

    arrived = exchange(outgoing, devices)
    change = crm(const, arrived, crm_field, crm_z, crm_x)
    returned = exchange(change, devices)
    dyn = pl.pallas_call(
        halo_kernel,
        in_specs=[VMEM] * 5,
        out_specs=VMEM,
        out_shape=f32(rows, col_dev),
        compiler_params=params(),
        cost_estimate=pl.CostEstimate(flops=10**8, bytes_accessed=2 * 10**6, transcendentals=0),
        name="halo",
    )(base, above, below, left, right)

    out = pl.pallas_call(
        final_kernel,
        in_specs=[VMEM] * 4,
        out_specs=pl.BlockSpec(memory_space=pl.ANY),
        out_shape=f32(rows * width_x, width_y),
        scratch_shapes=[
            pltpu.VMEM((rows * width_x, width_y), jnp.float32),
            pltpu.SemaphoreType.DMA((2,)),
        ],
        compiler_params=params(),
        name="final",
    )(dyn, returned, slot, up_map)
    return out.reshape(state.shape)


def solution(mesh):
    in_specs = (
        P(None, "gx", "gy"),
        P("gx", "gy"),
        P("gx", "gy"),
        P(),
        P(),
        P(),
        P(),
        P(None, ("gx", "gy")),
    )
    out_specs = P(None, "gx", "gy")
    return jax.shard_map(body, mesh=mesh, in_specs=in_specs, out_specs=out_specs, check_vma=False)
```
